32 devices in a mesh: groups: 2 (over x), clus: 16 (over z, y, core).
Axes of the slice: x: 2, y: 2, z: 4, core: 2. Of those that a mesh axis runs over, the one named last changes fastest.
Arguments:
- point_offsets: float32 [512, 3, 128], P(('groups', 'clus')), parts along dimension 0, may hold values from -0.3 to 0.3
- panel_normals: float32 [512, 3, 128], P(('groups', 'clus')), parts along dimension 0, may hold values from -0.5 to 0.5
- right_sketch: float32 [512, 64, 128], P(('groups', 'clus')), parts along dimension 0, may hold values from -6 to 6
- left_sketch: float32 [512, 64, 128], P(('groups', 'clus')), parts along dimension 0, may hold values from -6 to 6
- pair_count: int32 [32], P(('groups', 'clus')), parts along dimension 0, may hold values from 1 to 128, 1536 in all
- pair_rows: int32 [4096], P(('groups', 'clus')), parts along dimension 0, may hold values from 0 to 15
- pair_offset: int32 [4096, 1], P(('groups', 'clus')), parts along dimension 0, may hold values from 0 to 14; in each aligned block of 128 rows (0 to 127, 128 to 255, ...) at most 16 rows name the same one
- pair_cols: int32 [4096], P(('groups', 'clus')), parts along dimension 0, may hold values from 0 to 15, as said below
Outputs:
- row_sketch: float32 [512, 64, 128], P(('groups', 'clus')), parts along dimension 0
- col_sketch: float32 [512, 64, 128], P(('groups', 'clus')), parts along dimension 0
The draws below stay inside these ranges and needn't reach their ends.
There are 2 independent parts, one for each index of `groups`. The reference program is written for one: setup_inputs(seed, part) draws one part's arguments, and reference() takes and returns one part's arrays. A program takes and returns all parts, laid end to end along the dimension named above; each array names one. Nothing has to cross between parts.
Inputs may be any that keep to these rules, and one draw needn't show every extreme that they name: `pair_offset`: among the 128 slots of any one device no value appears more than 16 times; on some devices one value appears exactly 16 times. `pair_cols`: for every slot the first lattice coordinates of the centers of its row and column clusters differ by 2 or more (the pair is admissible).
All inputs are finite; a program needn't handle non-finite values. No bound on the sum of `pair_count` on one device may be relied on, other than what follows from the above.
Results may differ from the reference program's by a relative error of at most 0.0003.
Values sent between devices are 32-bit elements; how exact they have to be, the bound alone decides.
A program may use at most 64 MiB of HBM per device.

```python
import math
import jax
import jax.numpy as jnp
import numpy as np
from jax import lax

CP = 128
RANK = 32
CL_DEV = 16
PAIR_DEV = 128
OWNERS = 16
CLUSTERS = 256
PAIRS = 2048
MOST = 16
N_CLUS = 16


def slot_clusters(key):
    row_key = jax.random.fold_in(key, 11)
    pick_key = jax.random.fold_in(key, 12)
    step_key = jax.random.fold_in(key, 13)
    span = min(CL_DEV, 16)
    rows = jax.random.randint(row_key, (PAIRS,), 0, CL_DEV)
    closest = jax.random.randint(pick_key, (PAIRS,), 0, 2)
    stride = jax.random.randint(step_key, (PAIRS,), 2, span - 1)
    stride = jnp.where(closest > 0, 2, stride)
    base = rows - rows % span
    cols = base + (rows % span + stride) % span
    return (rows.astype(jnp.int32), cols.astype(jnp.int32))


def draw_pair_rows(key, part):
    shared = slot_clusters(key)
    return shared[0]


def draw_pair_cols(key, part):
    shared = slot_clusters(key)
    return shared[1]


def block_levels(stream_key, dims, pieces, smallest, largest):
    level = 1.0
    for dim, blocks in pieces:
        heights = jax.random.uniform(jax.random.fold_in(jax.random.fold_in(stream_key, 6), dim), (blocks,), jnp.float32, smallest / len(pieces), largest / len(pieces))
        level = level * jnp.repeat(jnp.exp(heights), dims[dim] // blocks).reshape((-1,) + (1,) * (len(dims) - 1 - dim))
    return level


def length_profile(number_of, total, limit, lean):
    loads = [(1 << 20) // math.isqrt(grade ** lean) + 1 for grade in range(2, number_of + 1)]
    surplus, holding = total - limit - (number_of - 1), [1] * (number_of - 1)
    while surplus > 0:
        movable = [i for i in range(number_of - 1) if holding[i] < limit]
        whole, budget = sum([loads[i] for i in movable]), surplus
        for i in movable:
            addition = min(limit - holding[i], max(1, budget * loads[i] // whole), surplus)
            holding[i] = holding[i] + addition
            surplus = surplus - addition
    return np.array([limit] + holding)


def ragged(key, amount, total, most, slope):
    if amount == 2:
        one = jax.random.randint(key, (), max(1, total - most), min(most, total - 1) + 1)
        return jnp.stack([one, total - one])
    sizes = jnp.asarray(length_profile(amount, total, most, slope), jnp.int32)
    twos = (amount - 1) // 2
    source_of, taker = sizes[1:1 + 2 * twos:2], sizes[2:2 + 2 * twos:2]
    room = jnp.minimum(source_of - 1, most - taker)
    moved = jax.random.randint(jax.random.fold_in(key, 1), (twos,), 0, 1 << 20) % (room + 1)
    sizes = sizes.at[1:1 + 2 * twos:2].set(source_of - moved).at[2:2 + 2 * twos:2].set(taker + moved)
    return sizes[jax.random.permutation(jax.random.fold_in(key, 2), amount)]


def deal_out(key, own, number, rows, amount, top, reach, slope):
    ranking = jax.random.permutation(key, amount)
    crowded, common = load_shares(amount, rows * top, reach, slope, True), load_shares(amount, rows * top, reach, slope, False)
    places = jnp.arange(amount)

    def named(lengths, offset_by):
        used = int((lengths > 0).sum())
        fixed = max(1, used // 4)
        shifted = fixed + (places - fixed + offset_by * (used - fixed)) % max(1, amount - fixed)
        return jnp.zeros((amount,), jnp.int32).at[ranking[jnp.where(places < fixed, places, shifted)]].set(jnp.asarray(lengths, jnp.int32))

    lengths = jnp.where(number % 4 == 0, named(crowded, number // 4), named(common, number - number // 4 - 1))
    mixed = jax.random.permutation(jax.random.fold_in(own, 3), amount)
    source_of, taker = mixed[0:amount // 2 * 2:2], mixed[1:amount // 2 * 2:2]
    margin = jnp.minimum(lengths[source_of] - 1, reach - lengths[taker]) // 2
    margin = jnp.where((source_of == ranking[0]) | (taker == ranking[0]) | (lengths[taker] == 0), 0, jnp.maximum(margin, 0))
    shifted = jax.random.randint(jax.random.fold_in(own, 4), (amount // 2,), 0, 1 << 20) % (margin + 1)
    lengths = lengths.at[source_of].add(-shifted).at[taker].add(shifted)
    items = jnp.searchsorted(jnp.cumsum(lengths), jnp.arange(rows * top), side="right").astype(jnp.int32)
    table = items.reshape(top, rows).T
    table = table[jax.random.permutation(jax.random.fold_in(own, 1), rows)]
    offset_by = jax.random.randint(jax.random.fold_in(own, 2), (rows, 1), 0, top)
    return jnp.take_along_axis(table, (jnp.arange(top)[None, :] + offset_by) % top, axis=1)


def load_shares(count, total, reach, skew, full):
    portions = [(1 << 20) // math.isqrt(rank ** skew) + 1 for rank in range(1, count + 1)]
    largest = reach if full else min(reach, max(-(-total // count), total * portions[0] // sum(portions)))
    least = 1 if total - largest >= count - 1 else 0
    given, spare = [largest] + [least] * (count - 1), total - largest - least * (count - 1)
    while spare > 0:
        candidates = [i for i in range(1, count) if given[i] < largest] or [i for i in range(1, count) if given[i] < reach]
        whole, remaining = sum([portions[i] for i in candidates]), spare
        for i in candidates:
            extra = min(reach - given[i], max(1, remaining * portions[i] // whole), spare)
            given[i] = given[i] + extra
            spare = spare - extra
    return np.array(given)


def centred(own_key, dims, spread, limit, split=(), kind=jnp.bfloat16):
    result = jax.random.normal(own_key, dims, jnp.float32) * spread
    if len(split) > 0:
        result = block_levels(own_key, dims, split, -0.22, 0.18) * result
    return jnp.clip(result, min=-limit, max=limit).astype(kind)


def setup_inputs(seed: int = 0, part: int = 0) -> dict:
    seeds = jax.random.split(jax.random.key(seed), 9)
    part_splits = jax.random.split(jax.random.fold_in(seeds[8], part), 9)
    point_offsets = jnp.clip(jax.random.uniform(part_splits[0], (CLUSTERS, 3, CP), jnp.float32, -0.3, 0.3) * block_levels(part_splits[0], (CLUSTERS, 3, CP), ((0, 16),), -0.4, 0.0), -0.3, 0.3)
    panel_normals = jnp.clip(jax.random.uniform(part_splits[1], (CLUSTERS, 3, CP), jnp.float32, -0.5, 0.5) * block_levels(part_splits[1], (CLUSTERS, 3, CP), ((0, 16),), -0.4, 0.0), -0.5, 0.5)
    right_sketch = centred(part_splits[2], (CLUSTERS, 2 * RANK, CP), 1.0, 6.0, ((0, 16),), jnp.float32)
    left_sketch = centred(part_splits[3], (CLUSTERS, 2 * RANK, CP), 1.0, 6.0, ((0, 16),), jnp.float32)
    pair_count = ragged(part_splits[4], OWNERS, PAIR_DEV * N_CLUS * 3 // 4, PAIR_DEV, 2).astype(jnp.int32)
    pair_rows = draw_pair_rows(jax.random.fold_in(jax.random.fold_in(seeds[8], part), 71), part)
    pair_offset_keys = jax.random.split(jax.random.fold_in(part_splits[6], 1), PAIRS // PAIR_DEV)
    pair_offset_turns = jax.random.permutation(jax.random.fold_in(part_splits[6], 3), PAIRS // PAIR_DEV)
    pair_offset = jax.vmap(lambda own, number: deal_out(jax.random.fold_in(part_splits[6], 2), own, number, PAIR_DEV, N_CLUS - 1, 1, MOST, 0))(pair_offset_keys, pair_offset_turns).reshape((PAIRS, 1))
    pair_cols = draw_pair_cols(jax.random.fold_in(jax.random.fold_in(seeds[8], part), 71), part)
    return {"point_offsets": point_offsets, "panel_normals": panel_normals, "right_sketch": right_sketch, "left_sketch": left_sketch, "pair_count": pair_count, "pair_rows": pair_rows, "pair_offset": pair_offset, "pair_cols": pair_cols}


wave_number = 8.0
precise = lax.Precision.HIGHEST

def centers_of(cluster_ids):
    return jnp.stack([cluster_ids % 16, cluster_ids // 16 % 8, cluster_ids // 128], axis=1).astype(jnp.float32)

def kernel_block(row_pts, row_nrm, col_pts, col_nrm):
    separation = row_pts[:, :, :, None] - col_pts[:, :, None, :]
    distance = jnp.sqrt(lax.optimization_barrier(jnp.sum(separation * separation, axis=1)))
    inverse = 1.0 / distance
    along_row = lax.optimization_barrier(jnp.sum(separation * row_nrm[:, :, :, None], axis=1))
    along_col = lax.optimization_barrier(jnp.sum(separation * col_nrm[:, :, None, :], axis=1))
    normal_dot = lax.optimization_barrier(jnp.sum(row_nrm[:, :, :, None] * col_nrm[:, :, None, :], axis=1))
    green_value = inverse / (4.0 * math.pi)
    cosine = jnp.cos(wave_number * distance)
    sine_part = jnp.sin(wave_number * distance)
    slope_real = green_value * (-cosine * inverse - wave_number * sine_part)
    slope_imag = green_value * (-sine_part * inverse + wave_number * cosine)
    double_real = -along_col * inverse * slope_real
    double_imag = -along_col * inverse * slope_imag
    curve_real = 3.0 * inverse * inverse - wave_number * wave_number
    curve_imag = -3.0 * wave_number * inverse
    second_real = green_value * (cosine * curve_real - sine_part * curve_imag)
    second_imag = green_value * (sine_part * curve_real + cosine * curve_imag)
    tangle = along_row * along_col * inverse * inverse
    hyper_real = -(tangle * second_real + normal_dot * inverse * slope_real)
    hyper_imag = -(tangle * second_imag + normal_dot * inverse * slope_imag)
    return (double_real - hyper_imag / wave_number, double_imag + hyper_real / wave_number)

def sketch_pair(kern_real, kern_imag, right_block, left_block):
    halves = right_block.shape[1] // 2
    real_right = jnp.einsum('bak,bik->bai', right_block, kern_real, precision=precise)
    imag_right = jnp.einsum('bak,bik->bai', right_block, kern_imag, precision=precise)
    row_part = jnp.concatenate([real_right[:, :halves] - imag_right[:, halves:], imag_right[:, :halves] + real_right[:, halves:]], axis=1)
    real_left = jnp.einsum('bai,bik->bak', left_block, kern_real, precision=precise)
    imag_left = jnp.einsum('bai,bik->bak', left_block, kern_imag, precision=precise)
    col_part = jnp.concatenate([real_left[:, :halves] + imag_left[:, halves:], real_left[:, halves:] - imag_left[:, :halves]], axis=1)
    return (row_part, col_part)

def reference(point_offsets, panel_normals, right_sketch, left_sketch, pair_count, pair_rows, pair_offset, pair_cols):
    points = point_offsets + centers_of(jnp.arange(CLUSTERS, dtype=jnp.int32))[:, :, None]
    slot_ids = jnp.arange(PAIRS, dtype=jnp.int32)
    owner_ids = slot_ids // PAIR_DEV
    is_live = (slot_ids % PAIR_DEV < pair_count[owner_ids]).astype(jnp.float32)
    row_ids = owner_ids * CL_DEV + pair_rows
    col_ids = (owner_ids + 1 + pair_offset[:, 0]) % OWNERS * CL_DEV + pair_cols

    def scan_step(running, block_data):
        row_block, col_block, weight = block_data
        kern_real, kern_imag = kernel_block(points[row_block], panel_normals[row_block], points[col_block], panel_normals[col_block])
        row_part, col_part = sketch_pair(kern_real, kern_imag, right_sketch[col_block], left_sketch[row_block])
        row_sum = running[0].at[row_block].add(row_part * weight[:, None, None])
        col_sum = running[1].at[col_block].add(col_part * weight[:, None, None])
        return ((row_sum, col_sum), None)
    zero_sums = jnp.zeros((CLUSTERS, 2 * RANK, CP), jnp.float32)
    blocks = (row_ids.reshape(-1, 8), col_ids.reshape(-1, 8), is_live.reshape(-1, 8))
    (row_sketch, col_sketch), unused = lax.scan(scan_step, (zero_sums, zero_sums), blocks)
    return (row_sketch, col_sketch)
```

```python
import math

import jax
import jax.numpy as jnp
import numpy as np
from jax import lax
from jax.experimental import pallas as pl
from jax.experimental.pallas import tpu as pltpu
from jax.sharding import PartitionSpec as P

wave_number = 8.0
precise = lax.Precision.HIGHEST


def centers_of(cluster_ids):
    return jnp.stack([cluster_ids % 16, cluster_ids // 16 % 8, cluster_ids // 128], axis=1).astype(
        jnp.float32
    )


def kernel_block(row_pts, row_nrm, col_pts, col_nrm):
    separation = row_pts[:, :, :, None] - col_pts[:, :, None, :]
    distance = jnp.sqrt(jnp.sum(separation * separation, axis=1))
    inverse = 1.0 / distance
    along_row = jnp.sum(separation * row_nrm[:, :, :, None], axis=1)
    along_col = jnp.sum(separation * col_nrm[:, :, None, :], axis=1)
    normal_dot = jnp.sum(row_nrm[:, :, :, None] * col_nrm[:, :, None, :], axis=1)
    green_value = inverse / (4.0 * math.pi)
    cosine = jnp.cos(wave_number * distance)
    sine_part = jnp.sin(wave_number * distance)
    slope_real = green_value * (-cosine * inverse - wave_number * sine_part)
    slope_imag = green_value * (-sine_part * inverse + wave_number * cosine)
    double_real = -along_col * inverse * slope_real
    double_imag = -along_col * inverse * slope_imag
    curve_real = 3.0 * inverse * inverse - wave_number * wave_number
    curve_imag = -3.0 * wave_number * inverse
    second_real = green_value * (cosine * curve_real - sine_part * curve_imag)
    second_imag = green_value * (sine_part * curve_real + cosine * curve_imag)
    tangle = along_row * along_col * inverse * inverse
    hyper_real = -(tangle * second_real + normal_dot * inverse * slope_real)
    hyper_imag = -(tangle * second_imag + normal_dot * inverse * slope_imag)
    return (double_real - hyper_imag / wave_number, double_imag + hyper_real / wave_number)


def sketch_pair(kern_real, kern_imag, right_block, left_block):
    halves = right_block.shape[1] // 2
    real_right = jnp.einsum("bak,bik->bai", right_block, kern_real, precision=precise)
    imag_right = jnp.einsum("bak,bik->bai", right_block, kern_imag, precision=precise)
    row_part = jnp.concatenate(
        [
            real_right[:, :halves] - imag_right[:, halves:],
            imag_right[:, :halves] + real_right[:, halves:],
        ],
        axis=1,
    )
    real_left = jnp.einsum("bai,bik->bak", left_block, kern_real, precision=precise)
    imag_left = jnp.einsum("bai,bik->bak", left_block, kern_imag, precision=precise)
    col_part = jnp.concatenate(
        [
            real_left[:, :halves] + imag_left[:, halves:],
            real_left[:, halves:] - imag_left[:, :halves],
        ],
        axis=1,
    )
    return (row_part, col_part)


def exchange_shards(
    point_offsets,
    panel_normals,
    right_sketch,
    left_sketch,
    pair_count,
    pair_rows,
    pair_offset,
    pair_cols,
):
    owners = lax.axis_size("clus")
    position = lax.axis_index("clus")
    cl_dev, width, panels = right_sketch.shape
    slots = pair_rows.shape[0]
    per_peer = max(2, 2 * slots // owners)
    slot_total = owners * per_peer
    local_ids = position * cl_dev + jnp.arange(cl_dev, dtype=jnp.int32)
    cluster_range = jnp.arange(cl_dev, dtype=jnp.int32)
    points = point_offsets + centers_of(local_ids)[:, :, None]
    live_count = pair_count[0]
    slot_index = jnp.arange(slots, dtype=jnp.int32)
    is_live = slot_index < live_count
    target = (position + 1 + pair_offset[:, 0]) % owners
    peer_hits = (target[:, None] == jnp.arange(owners, dtype=jnp.int32)[None, :]).astype(jnp.int32)
    peer_rank = jnp.sum(jnp.cumsum(peer_hits, axis=0) * peer_hits, axis=1) - 1
    send_pos = target * per_peer + peer_rank
    col_global = target * cl_dev + pair_cols
    zero_buffer = jnp.zeros((slot_total, width, panels), jnp.float32)
    zero_local = jnp.zeros((cl_dev, width, panels), jnp.float32)
    col_tags = (
        jnp.full((slot_total,), -1, jnp.int32).at[send_pos].set(jnp.where(is_live, pair_cols, -1))
    )
    incoming = lax.all_to_all(
        col_tags.reshape(owners, per_peer), "clus", split_axis=0, concat_axis=0, tiled=True
    ).reshape(slot_total)
    picked = jnp.maximum(incoming, 0)
    got_pts, got_nrm, got_right = (
        lax.all_to_all(
            point_offsets[picked].reshape(owners, per_peer, 3, panels),
            "clus",
            split_axis=0,
            concat_axis=0,
            tiled=True,
        ),
        lax.all_to_all(
            panel_normals[picked].reshape(owners, per_peer, 3, panels),
            "clus",
            split_axis=0,
            concat_axis=0,
            tiled=True,
        ),
        lax.all_to_all(
            right_sketch[picked].reshape(owners, per_peer, width, panels),
            "clus",
            split_axis=0,
            concat_axis=0,
            tiled=True,
        ),
    )
    got_pts = got_pts.reshape(slot_total, 3, panels)
    got_nrm = got_nrm.reshape(slot_total, 3, panels)
    got_right = got_right.reshape(slot_total, width, panels)

    def owner_step(block_turn, running):
        row_sum, outgoing = running
        block_index = block_turn * 8 + jnp.arange(8, dtype=jnp.int32)
        weight = (block_index < live_count).astype(jnp.float32)
        slot_at = lax.dynamic_slice_in_dim(send_pos, block_turn * 8, 8)
        row_local = lax.dynamic_slice_in_dim(pair_rows, block_turn * 8, 8)
        col_block = lax.dynamic_slice_in_dim(col_global, block_turn * 8, 8)
        col_pts = got_pts[slot_at] + centers_of(col_block)[:, :, None]
        kern_real, kern_imag = kernel_block(
            points[row_local], panel_normals[row_local], col_pts, got_nrm[slot_at]
        )
        row_part, col_part = sketch_pair(
            kern_real, kern_imag, got_right[slot_at], left_sketch[row_local]
        )
        select = (row_local[:, None] == cluster_range[None, :]).astype(jnp.float32) * weight[
            :, None
        ]
        row_sum = row_sum + jnp.einsum("bl,bak->lak", select, row_part, precision=precise)
        outgoing = outgoing.at[slot_at].add(col_part * weight[:, None, None])
        return (row_sum, outgoing)

    turn_count = (live_count + 7) // 8
    row_sum, outgoing = lax.fori_loop(0, turn_count, owner_step, (zero_local, zero_buffer))
    returned = lax.all_to_all(
        outgoing.reshape(owners, per_peer, width, panels),
        "clus",
        split_axis=0,
        concat_axis=0,
        tiled=True,
    ).reshape(slot_total, width, panels)
    select = (incoming[:, None] == cluster_range[None, :]).astype(jnp.float32)
    col_sum = jnp.einsum("sl,sak->lak", select, returned, precision=precise)
    return (row_sum, col_sum)


geometry_rows = 8
unroll = 2
vmem_budget = 40 * 2**20
kernel_scale = wave_number * wave_number / (12.0 * math.pi)


def phase_coefficients():
    def fit(function, degree):
        series = np.polynomial.chebyshev.Chebyshev.interpolate(function, degree, domain=[0.0, 0.25])
        return [float(c) for c in series.convert(kind=np.polynomial.Polynomial).coef]

    def sine_ratio(z):
        return math.sqrt(2.0) * math.pi * np.sinc(np.sqrt(z))

    def cosine(z):
        return math.sqrt(2.0) * np.cos(math.pi * np.sqrt(z))

    return fit(sine_ratio, 3), fit(cosine, 4)


sine_terms, cosine_terms = phase_coefficients()


def horner(terms, z):
    value = terms[-1] * z + terms[-2]
    for term in terms[-3::-1]:
        value = value * z + term
    return value


def high_low(x):
    high = lax.reduce_precision(x, 8, 7)
    return high, lax.reduce_precision(x - high, 8, 7)


def row_features(offsets, normals):
    cl_dev, _, panels = offsets.shape
    x = wave_number * jnp.swapaxes(offsets, 1, 2)
    n = jnp.swapaxes(normals, 1, 2)
    zero3 = jnp.zeros_like(x)
    zero1 = zero3[:, :, :1]
    one1 = jnp.ones_like(zero1)

    def form(columns, constant):
        high, low = high_low(jnp.concatenate(columns, axis=2))
        c_high, rest = high_low(constant)
        c_low = lax.reduce_precision(constant - c_high - rest, 8, 7)
        tail = jnp.concatenate([c_high, rest, c_low, zero3, zero1, zero1], axis=2)
        return jnp.concatenate([high, high, high, low, low, tail], axis=2)

    square = form([-2.0 * x, zero3, one1, zero1], jnp.sum(x * x, axis=2, keepdims=True))
    along_col = form([zero3, x, zero1, -one1], zero1)
    along_row = form([-n, zero3, zero1, zero1], jnp.sum(x * n, axis=2, keepdims=True))
    normal_dot = form([zero3, n, zero1, zero1], zero1)
    top = jnp.concatenate([square, along_col], axis=2)
    bottom = jnp.concatenate([along_row, normal_dot], axis=2)
    return jnp.concatenate([top, bottom], axis=1).astype(jnp.bfloat16)


def left_operand(left):
    halves = left.shape[1] // 2
    real, imag = left[:, :halves], left[:, halves:]
    stacked = jnp.concatenate(
        [jnp.concatenate([real, imag], axis=2), jnp.concatenate([imag, -real], axis=2)], axis=1
    )
    high, low = high_low(stacked)
    return jnp.concatenate([high, low], axis=1).astype(jnp.bfloat16)


def split_two(x):
    high = x.astype(jnp.bfloat16)
    return high, (x - high.astype(jnp.float32)).astype(jnp.bfloat16)


def pair_parts(features, left, column, width, shift):
    panels = column.shape[1]
    halves = width // 2
    geometry = column[width:]
    index = lax.broadcasted_iota(jnp.int32, geometry.shape, 0)
    move = jnp.where(
        index == 0, shift[0], jnp.where(index == 1, shift[1], jnp.where(index == 2, shift[2], 0.0))
    )
    base = jnp.where(index < 3, wave_number, 1.0) * (geometry + move)
    y = [base[i : i + 1] for i in range(3)]
    m = [base[i : i + 1] for i in range(3, 6)]
    square = y[0] * y[0] + y[1] * y[1] + y[2] * y[2]
    inner = y[0] * m[0] + y[1] * m[1] + y[2] * m[2]
    full = jnp.where(index == 6, square, jnp.where(index == 7, inner, base))
    high = full.astype(jnp.bfloat16).astype(jnp.float32)
    rest = full - high
    middle = rest.astype(jnp.bfloat16).astype(jnp.float32)
    low = rest - middle
    stack = jnp.concatenate([high, middle, low, high, middle, jnp.ones_like(high)], axis=0).astype(
        jnp.bfloat16
    )
    empty = jnp.zeros_like(stack)
    operand = jnp.concatenate(
        [jnp.concatenate([stack, empty], axis=1), jnp.concatenate([empty, stack], axis=1)], axis=0
    )
    forms = jnp.dot(features, operand, preferred_element_type=jnp.float32)

    pieces = []
    chunk = 32
    magic = 1.5 * 2.0**23
    for start in range(0, panels, chunk):
        r2 = forms[start : start + chunk, :panels]
        along_col = forms[start : start + chunk, panels:]
        along_row = forms[panels + start : panels + start + chunk, :panels]
        normal_dot = forms[panels + start : panels + start + chunk, panels:]
        inverse = lax.rsqrt(r2)
        turns = (r2 * inverse) * (0.5 / math.pi)
        turns = turns - ((turns + magic) - magic)
        z = turns * turns
        sine_half = turns * horner(sine_terms, z)
        cosine_half = horner(cosine_terms, z)
        weight = 3.0 * (inverse * inverse)
        scaled = sine_half * weight
        sine_w = scaled * cosine_half
        cosine_w = weight - scaled * sine_half
        both = along_col * along_row
        inner_term = normal_dot - both * weight
        real = inner_term + along_col * inverse
        imag = inverse * (inner_term + both) - along_col
        pieces.append(
            split_two(cosine_w * real - sine_w * imag) + split_two(cosine_w * imag + sine_w * real)
        )
    real_high, real_low, imag_high, imag_low = [
        jnp.concatenate([piece[q] for piece in pieces], axis=0) for q in range(4)
    ]
    left_rhs = jnp.concatenate(
        [
            jnp.concatenate([real_high, real_low], axis=1),
            jnp.concatenate([imag_high, imag_low], axis=1),
        ],
        axis=0,
    )
    right_rhs = jnp.concatenate(
        [
            jnp.concatenate([real_high, imag_high], axis=1),
            jnp.concatenate([real_low, imag_low], axis=1),
        ],
        axis=0,
    )
    w_high, w_low = split_two(column[:width])

    def complex_rows(block):
        real, imag = block[:halves], block[halves:]
        return [jnp.concatenate([real, -imag], axis=1), jnp.concatenate([imag, real], axis=1)]

    right = jnp.concatenate(complex_rows(w_high) + complex_rows(w_low), axis=0)
    row_out = lax.dot_general(
        right, right_rhs, (((1,), (1,)), ((), ())), preferred_element_type=jnp.float32
    )
    col_out = jnp.dot(left, left_rhs, preferred_element_type=jnp.float32)

    def fold(out):
        return (
            out[:width, :panels]
            + out[:width, panels:]
            + (out[width:, :panels] + out[width:, panels:])
        )

    return fold(row_out), fold(col_out)


def pair_kernel(
    live_ref, row_ref, global_row_ref, col_ref, features_ref, left_ref, column_ref, row_out, col_out
):
    row_out[...] = jnp.zeros_like(row_out)
    width = row_out.shape[1]

    def clear(i, carry):
        col_out[i] = jnp.zeros(col_out.shape[1:], jnp.float32)
        return carry

    lax.fori_loop(0, col_out.shape[0], clear, 0)
    live = live_ref[0]

    def center(c):
        return (c & 15, (c >> 4) & 7, c >> 7)

    def turn(step, carry):
        done = []
        for k in range(unroll):
            slot = step * unroll + k
            row = row_ref[slot]
            col = col_ref[slot]
            shift = [
                (b - a).astype(jnp.float32)
                for a, b in zip(center(global_row_ref[slot]), center(col))
            ]
            parts = pair_parts(features_ref[row], left_ref[row], column_ref[col], width, shift)
            scale = jnp.where(slot < live, kernel_scale, 0.0)
            done.append((row, col, parts[0] * scale, parts[1] * scale))
        for row, col, row_part, col_part in done:
            row_out[row] += row_part
            col_out[col] += col_part
        return carry

    lax.fori_loop(0, (live + unroll - 1) // unroll, turn, 0)


def sketch_pairs(live, rows, global_rows, cols, features, left, columns, width):
    cl_dev = features.shape[0]
    clusters, _, panels = columns.shape
    return pl.pallas_call(
        pair_kernel,
        grid_spec=pltpu.PrefetchScalarGridSpec(
            num_scalar_prefetch=4,
            in_specs=[pl.BlockSpec(memory_space=pltpu.VMEM)] * 3,
            out_specs=[pl.BlockSpec(memory_space=pltpu.VMEM)] * 2,
        ),
        out_shape=(
            jax.ShapeDtypeStruct((cl_dev, width, panels), jnp.float32),
            jax.ShapeDtypeStruct((clusters, width, panels), jnp.float32),
        ),
        compiler_params=pltpu.CompilerParams(vmem_limit_bytes=vmem_budget),
        name="pair_sketches",
    )(live, rows, global_rows, cols, features, left, columns)


def gather_shards(
    point_offsets,
    panel_normals,
    right_sketch,
    left_sketch,
    pair_count,
    pair_rows,
    pair_offset,
    pair_cols,
):
    owners = lax.axis_size("clus")
    position = lax.axis_index("clus")
    cl_dev, width, panels = right_sketch.shape
    spare = jnp.zeros((cl_dev, geometry_rows - 6, panels), jnp.float32)
    packed = jnp.concatenate([right_sketch, point_offsets, panel_normals, spare], axis=1)
    columns = lax.all_gather(packed, "clus", axis=0, tiled=True)
    target = (position + 1 + pair_offset[:, 0]) % owners
    row_sum, outgoing = sketch_pairs(
        pair_count,
        pair_rows,
        position * cl_dev + pair_rows,
        target * cl_dev + pair_cols,
        row_features(point_offsets, panel_normals),
        left_operand(left_sketch),
        columns,
        width,
    )
    col_sum = lax.psum_scatter(outgoing, "clus", scatter_dimension=0, tiled=True)
    return (row_sum, col_sum)


def shards(
    point_offsets,
    panel_normals,
    right_sketch,
    left_sketch,
    pair_count,
    pair_rows,
    pair_offset,
    pair_cols,
):
    cl_dev, width, panels = right_sketch.shape
    held = lax.axis_size("clus") * cl_dev * (2 * width + geometry_rows) * panels * 4
    plan = gather_shards if held + 2**23 <= vmem_budget else exchange_shards
    return plan(
        point_offsets,
        panel_normals,
        right_sketch,
        left_sketch,
        pair_count,
        pair_rows,
        pair_offset,
        pair_cols,
    )


def solution(mesh):
    return jax.shard_map(
        shards,
        mesh=mesh,
        in_specs=(
            P(("groups", "clus"), None, None),
            P(("groups", "clus"), None, None),
            P(("groups", "clus"), None, None),
            P(("groups", "clus"), None, None),
            P(("groups", "clus")),
            P(("groups", "clus")),
            P(("groups", "clus"), None),
            P(("groups", "clus")),
        ),
        out_specs=(P(("groups", "clus"), None, None), P(("groups", "clus"), None, None)),
        check_vma=False,
    )
```

```python
import functools
import math

import jax
import jax.numpy as jnp
import numpy as np
from jax import lax
from jax.experimental import pallas as pl
from jax.experimental.pallas import tpu as pltpu
from jax.sharding import PartitionSpec as P

wave_number = 8.0
precise = lax.Precision.HIGHEST


def centers_of(cluster_ids):
    return jnp.stack([cluster_ids % 16, cluster_ids // 16 % 8, cluster_ids // 128], axis=1).astype(
        jnp.float32
    )


def kernel_block(row_pts, row_nrm, col_pts, col_nrm):
    separation = row_pts[:, :, :, None] - col_pts[:, :, None, :]
    distance = jnp.sqrt(jnp.sum(separation * separation, axis=1))
    inverse = 1.0 / distance
    along_row = jnp.sum(separation * row_nrm[:, :, :, None], axis=1)
    along_col = jnp.sum(separation * col_nrm[:, :, None, :], axis=1)
    normal_dot = jnp.sum(row_nrm[:, :, :, None] * col_nrm[:, :, None, :], axis=1)
    green_value = inverse / (4.0 * math.pi)
    cosine = jnp.cos(wave_number * distance)
    sine_part = jnp.sin(wave_number * distance)
    slope_real = green_value * (-cosine * inverse - wave_number * sine_part)
    slope_imag = green_value * (-sine_part * inverse + wave_number * cosine)
    double_real = -along_col * inverse * slope_real
    double_imag = -along_col * inverse * slope_imag
    curve_real = 3.0 * inverse * inverse - wave_number * wave_number
    curve_imag = -3.0 * wave_number * inverse
    second_real = green_value * (cosine * curve_real - sine_part * curve_imag)
    second_imag = green_value * (sine_part * curve_real + cosine * curve_imag)
    tangle = along_row * along_col * inverse * inverse
    hyper_real = -(tangle * second_real + normal_dot * inverse * slope_real)
    hyper_imag = -(tangle * second_imag + normal_dot * inverse * slope_imag)
    return (double_real - hyper_imag / wave_number, double_imag + hyper_real / wave_number)


def sketch_pair(kern_real, kern_imag, right_block, left_block):
    halves = right_block.shape[1] // 2
    real_right = jnp.einsum("bak,bik->bai", right_block, kern_real, precision=precise)
    imag_right = jnp.einsum("bak,bik->bai", right_block, kern_imag, precision=precise)
    row_part = jnp.concatenate(
        [
            real_right[:, :halves] - imag_right[:, halves:],
            imag_right[:, :halves] + real_right[:, halves:],
        ],
        axis=1,
    )
    real_left = jnp.einsum("bai,bik->bak", left_block, kern_real, precision=precise)
    imag_left = jnp.einsum("bai,bik->bak", left_block, kern_imag, precision=precise)
    col_part = jnp.concatenate(
        [
            real_left[:, :halves] + imag_left[:, halves:],
            real_left[:, halves:] - imag_left[:, :halves],
        ],
        axis=1,
    )
    return (row_part, col_part)


def exchange_shards(
    point_offsets,
    panel_normals,
    right_sketch,
    left_sketch,
    pair_count,
    pair_rows,
    pair_offset,
    pair_cols,
):
    owners = lax.axis_size("clus")
    position = lax.axis_index("clus")
    cl_dev, width, panels = right_sketch.shape
    slots = pair_rows.shape[0]
    per_peer = max(2, 2 * slots // owners)
    slot_total = owners * per_peer
    local_ids = position * cl_dev + jnp.arange(cl_dev, dtype=jnp.int32)
    cluster_range = jnp.arange(cl_dev, dtype=jnp.int32)
    points = point_offsets + centers_of(local_ids)[:, :, None]
    live_count = pair_count[0]
    slot_index = jnp.arange(slots, dtype=jnp.int32)
    is_live = slot_index < live_count
    target = (position + 1 + pair_offset[:, 0]) % owners
    peer_hits = (target[:, None] == jnp.arange(owners, dtype=jnp.int32)[None, :]).astype(jnp.int32)
    peer_rank = jnp.sum(jnp.cumsum(peer_hits, axis=0) * peer_hits, axis=1) - 1
    send_pos = target * per_peer + peer_rank
    col_global = target * cl_dev + pair_cols
    zero_buffer = jnp.zeros((slot_total, width, panels), jnp.float32)
    zero_local = jnp.zeros((cl_dev, width, panels), jnp.float32)
    col_tags = (
        jnp.full((slot_total,), -1, jnp.int32).at[send_pos].set(jnp.where(is_live, pair_cols, -1))
    )
    incoming = lax.all_to_all(
        col_tags.reshape(owners, per_peer), "clus", split_axis=0, concat_axis=0, tiled=True
    ).reshape(slot_total)
    picked = jnp.maximum(incoming, 0)
    got_pts, got_nrm, got_right = (
        lax.all_to_all(
            point_offsets[picked].reshape(owners, per_peer, 3, panels),
            "clus",
            split_axis=0,
            concat_axis=0,
            tiled=True,
        ),
        lax.all_to_all(
            panel_normals[picked].reshape(owners, per_peer, 3, panels),
            "clus",
            split_axis=0,
            concat_axis=0,
            tiled=True,
        ),
        lax.all_to_all(
            right_sketch[picked].reshape(owners, per_peer, width, panels),
            "clus",
            split_axis=0,
            concat_axis=0,
            tiled=True,
        ),
    )
    got_pts = got_pts.reshape(slot_total, 3, panels)
    got_nrm = got_nrm.reshape(slot_total, 3, panels)
    got_right = got_right.reshape(slot_total, width, panels)

    def owner_step(block_turn, running):
        row_sum, outgoing = running
        block_index = block_turn * 8 + jnp.arange(8, dtype=jnp.int32)
        weight = (block_index < live_count).astype(jnp.float32)
        slot_at = lax.dynamic_slice_in_dim(send_pos, block_turn * 8, 8)
        row_local = lax.dynamic_slice_in_dim(pair_rows, block_turn * 8, 8)
        col_block = lax.dynamic_slice_in_dim(col_global, block_turn * 8, 8)
        col_pts = got_pts[slot_at] + centers_of(col_block)[:, :, None]
        kern_real, kern_imag = kernel_block(
            points[row_local], panel_normals[row_local], col_pts, got_nrm[slot_at]
        )
        row_part, col_part = sketch_pair(
            kern_real, kern_imag, got_right[slot_at], left_sketch[row_local]
        )
        select = (row_local[:, None] == cluster_range[None, :]).astype(jnp.float32) * weight[
            :, None
        ]
        row_sum = row_sum + jnp.einsum("bl,bak->lak", select, row_part, precision=precise)
        outgoing = outgoing.at[slot_at].add(col_part * weight[:, None, None])
        return (row_sum, outgoing)

    turn_count = (live_count + 7) // 8
    row_sum, outgoing = lax.fori_loop(0, turn_count, owner_step, (zero_local, zero_buffer))
    returned = lax.all_to_all(
        outgoing.reshape(owners, per_peer, width, panels),
        "clus",
        split_axis=0,
        concat_axis=0,
        tiled=True,
    ).reshape(slot_total, width, panels)
    select = (incoming[:, None] == cluster_range[None, :]).astype(jnp.float32)
    col_sum = jnp.einsum("sl,sak->lak", select, returned, precision=precise)
    return (row_sum, col_sum)


geometry_rows = 8
unroll = 2
vmem_budget = 40 * 2**20
kernel_scale = wave_number * wave_number / (12.0 * math.pi)


def phase_coefficients():
    def fit(function, degree):
        series = np.polynomial.chebyshev.Chebyshev.interpolate(function, degree, domain=[0.0, 0.25])
        return [float(c) for c in series.convert(kind=np.polynomial.Polynomial).coef]

    def sine_ratio(z):
        return math.sqrt(2.0) * math.pi * np.sinc(np.sqrt(z))

    def cosine(z):
        return math.sqrt(2.0) * np.cos(math.pi * np.sqrt(z))

    return fit(sine_ratio, 3), fit(cosine, 4)


sine_terms, cosine_terms = phase_coefficients()


def horner(terms, z):
    value = terms[-1] * z + terms[-2]
    for term in terms[-3::-1]:
        value = value * z + term
    return value


def split_two(x):
    high = x.astype(jnp.bfloat16)
    return high, (x - high.astype(jnp.float32)).astype(jnp.bfloat16)


def rounded(x):
    return x.astype(jnp.bfloat16).astype(jnp.float32)


def row_features(geometry):
    index = lax.broadcasted_iota(jnp.int32, geometry.shape, 0)
    x = [wave_number * geometry[i : i + 1] for i in range(3)]
    n = [geometry[i : i + 1] for i in range(3, 6)]
    zero = jnp.zeros_like(x[0])
    one = zero + 1.0

    def rows(parts):
        block = jnp.zeros_like(geometry)
        for i, part in parts.items():
            block = jnp.where(index == i, part, block)
        return block

    def form(parts, constant):
        block = rows(parts)
        high = rounded(block)
        low = block - high
        c_high = rounded(constant)
        c_middle = rounded(constant - c_high)
        tail = rows({0: c_high, 1: c_middle, 2: constant - c_high - c_middle})
        return jnp.concatenate([high, high, high, low, low, tail], axis=0)

    square = form(
        {0: -2.0 * x[0], 1: -2.0 * x[1], 2: -2.0 * x[2], 6: one},
        x[0] * x[0] + x[1] * x[1] + x[2] * x[2],
    )
    along_col = form({3: x[0], 4: x[1], 5: x[2], 7: -one}, zero)
    along_row = form({0: -n[0], 1: -n[1], 2: -n[2]}, x[0] * n[0] + x[1] * n[1] + x[2] * n[2])
    normal_dot = form({3: n[0], 4: n[1], 5: n[2]}, zero)
    empty = jnp.zeros((32, geometry.shape[1]), jnp.float32)
    left = jnp.concatenate([square, along_col, empty], axis=0)
    right = jnp.concatenate([along_row, normal_dot, empty], axis=0)
    both = jnp.concatenate([left.T, right.T], axis=0)
    return both[:, :96].astype(jnp.bfloat16)


def left_operand(left):
    halves = left.shape[0] // 2

    def complex_rows(block):
        real, imag = block[:halves], block[halves:]
        return [jnp.concatenate([real, imag], axis=1), jnp.concatenate([imag, -real], axis=1)]

    high, low = split_two(left)
    return jnp.concatenate(complex_rows(high) + complex_rows(low), axis=0)


def pair_parts(features, left, column, width, shift):
    panels = column.shape[1]
    halves = width // 2
    geometry = column[width:]
    index = lax.broadcasted_iota(jnp.int32, geometry.shape, 0)
    move = jnp.where(
        index == 0, shift[0], jnp.where(index == 1, shift[1], jnp.where(index == 2, shift[2], 0.0))
    )
    base = jnp.where(index < 3, wave_number, 1.0) * (geometry + move)
    y = [base[i : i + 1] for i in range(3)]
    m = [base[i : i + 1] for i in range(3, 6)]
    square = y[0] * y[0] + y[1] * y[1] + y[2] * y[2]
    inner = y[0] * m[0] + y[1] * m[1] + y[2] * m[2]
    full = jnp.where(index == 6, square, jnp.where(index == 7, inner, base))
    high = full.astype(jnp.bfloat16).astype(jnp.float32)
    rest = full - high
    middle = rest.astype(jnp.bfloat16).astype(jnp.float32)
    low = rest - middle
    stack = jnp.concatenate([high, middle, low, high, middle, jnp.ones_like(high)], axis=0).astype(
        jnp.bfloat16
    )
    empty = jnp.zeros_like(stack)
    operand = jnp.concatenate(
        [jnp.concatenate([stack, empty], axis=1), jnp.concatenate([empty, stack], axis=1)], axis=0
    )
    forms = jnp.dot(features, operand, preferred_element_type=jnp.float32)

    pieces = []
    chunk = 32
    magic = 1.5 * 2.0**23
    for start in range(0, panels, chunk):
        r2 = forms[start : start + chunk, :panels]
        along_col = forms[start : start + chunk, panels:]
        along_row = forms[panels + start : panels + start + chunk, :panels]
        normal_dot = forms[panels + start : panels + start + chunk, panels:]
        inverse = lax.rsqrt(r2)
        turns = (r2 * inverse) * (0.5 / math.pi)
        turns = turns - ((turns + magic) - magic)
        z = turns * turns
        sine_half = turns * horner(sine_terms, z)
        cosine_half = horner(cosine_terms, z)
        weight = 3.0 * (inverse * inverse)
        scaled = sine_half * weight
        sine_w = scaled * cosine_half
        cosine_w = weight - scaled * sine_half
        both = along_col * along_row
        inner_term = normal_dot - both * weight
        real = inner_term + along_col * inverse
        imag = inverse * (inner_term + both) - along_col
        pieces.append(
            split_two(cosine_w * real - sine_w * imag) + split_two(cosine_w * imag + sine_w * real)
        )
    real_high, real_low, imag_high, imag_low = [
        jnp.concatenate([piece[q] for piece in pieces], axis=0) for q in range(4)
    ]
    left_rhs = jnp.concatenate(
        [
            jnp.concatenate([real_high, real_low], axis=1),
            jnp.concatenate([imag_high, imag_low], axis=1),
        ],
        axis=0,
    )
    right_rhs = jnp.concatenate(
        [
            jnp.concatenate([real_high, imag_high], axis=1),
            jnp.concatenate([real_low, imag_low], axis=1),
        ],
        axis=0,
    )
    w_high, w_low = split_two(column[:width])

    def complex_rows(block):
        real, imag = block[:halves], block[halves:]
        return [jnp.concatenate([real, -imag], axis=1), jnp.concatenate([imag, real], axis=1)]

    right = jnp.concatenate(complex_rows(w_high) + complex_rows(w_low), axis=0)
    row_out = lax.dot_general(
        right, right_rhs, (((1,), (1,)), ((), ())), preferred_element_type=jnp.float32
    )
    col_out = jnp.dot(left, left_rhs, preferred_element_type=jnp.float32)

    def fold(out):
        return (
            out[:width, :panels]
            + out[:width, panels:]
            + (out[width:, :panels] + out[width:, panels:])
        )

    return fold(row_out), fold(col_out)


def pair_kernel(
    live_ref, row_ref, global_row_ref, col_ref, features_ref, left_ref, column_ref, row_out, col_out
):
    row_out[...] = jnp.zeros_like(row_out)
    width = row_out.shape[1]

    def clear(i, carry):
        col_out[i] = jnp.zeros(col_out.shape[1:], jnp.float32)
        return carry

    lax.fori_loop(0, col_out.shape[0], clear, 0)
    live = live_ref[0]

    def center(c):
        return (c & 15, (c >> 4) & 7, c >> 7)

    def turn(step, carry):
        done = []
        for k in range(unroll):
            slot = step * unroll + k
            row = row_ref[slot]
            col = col_ref[slot]
            shift = [
                (b - a).astype(jnp.float32)
                for a, b in zip(center(global_row_ref[slot]), center(col))
            ]
            parts = pair_parts(features_ref[row], left_ref[row], column_ref[col], width, shift)
            scale = jnp.where(slot < live, kernel_scale, 0.0)
            done.append((row, col, parts[0] * scale, parts[1] * scale))
        for row, col, row_part, col_part in done:
            row_out[row] += row_part
            col_out[col] += col_part
        return carry

    lax.fori_loop(0, (live + unroll - 1) // unroll, turn, 0)


def sketch_pairs(live, rows, global_rows, cols, features, left, columns, width):
    cl_dev = features.shape[0]
    clusters, _, panels = columns.shape
    return pl.pallas_call(
        pair_kernel,
        grid_spec=pltpu.PrefetchScalarGridSpec(
            num_scalar_prefetch=4,
            in_specs=[pl.BlockSpec(memory_space=pltpu.VMEM)] * 3,
            out_specs=[pl.BlockSpec(memory_space=pltpu.VMEM)] * 2,
        ),
        out_shape=(
            jax.ShapeDtypeStruct((cl_dev, width, panels), jnp.float32),
            jax.ShapeDtypeStruct((clusters, width, panels), jnp.float32),
        ),
        compiler_params=pltpu.CompilerParams(vmem_limit_bytes=vmem_budget),
        name="pair_sketches",
    )(live, rows, global_rows, cols, features, left, columns)


def neighbours(line):
    me = lax.axis_index("clus")
    core, side, place = me % 2, me // 2 % 2, me // 4
    return me, core, side, place


def index_of(place, side, core):
    return place * 4 + side * 2 + core


def greet(line, place, side, core):
    barrier = pltpu.get_barrier_semaphore()

    def call(target):
        pl.semaphore_signal(barrier, inc=1, device_id={"clus": target})

    call(index_of(place, side, 1 - core))
    call(index_of(place, 1 - side, core))

    @pl.when(place > 0)
    def _():
        call(index_of(place - 1, side, core))

    @pl.when(place < line - 1)
    def _():
        call(index_of(place + 1, side, core))

    pl.semaphore_wait(barrier, 2 + jnp.minimum(place, 1) + jnp.minimum(line - 1 - place, 1))


def gather_kernel(
    line,
    x_ref,
    sketch_ref,
    out_ref,
    features_ref,
    left_ref,
    send_sem,
    recv_sem,
    local_sem,
):
    me, core, side, place = neighbours(line)
    size = x_ref.shape[0]

    def block(q):
        return out_ref.at[pl.ds(pl.multiple_of(q * size, size), size)]

    def copy(q, target, index):
        return pltpu.make_async_remote_copy(
            src_ref=block(q),
            dst_ref=block(q),
            send_sem=send_sem.at[index],
            recv_sem=recv_sem.at[q],
            device_id={"clus": target},
        )

    def arrived(q):
        copy(q, index_of(place, side, 1 - core), 0).wait_recv()

    mine = pltpu.make_async_copy(x_ref, block(me), local_sem)
    mine.start()
    greet(line, place, side, core)
    mine.wait()

    sends = []

    def send(condition, q, target):
        sends.append((condition, q, target))
        index = len(sends) - 1

        @pl.when(condition)
        def _():
            copy(q, target, index).start()

    always = place >= 0
    sibling = index_of(place, side, 1 - core)
    across = index_of(place, 1 - side, core)
    down = index_of(place - 1, side, core)
    up = index_of(place + 1, side, core)

    def pass_on(q, here, forward, target):
        send(here & forward, q, target)
        send(here, q, across)
        send(here, q, sibling)

    def relay(q, here):
        @pl.when(here)
        def _():
            arrived(q)

        send(here, q, sibling)

    send(place < line - 1, me, up)
    send(place > 0, me, down)
    send(always, me, across)
    send(always, me, sibling)
    width = sketch_ref.shape[1]

    def prepare(i, carry):
        features_ref[i] = row_features(x_ref[i][width:])
        left_ref[i] = left_operand(sketch_ref[i])
        return carry

    lax.fori_loop(0, size, prepare, 0)
    for step in range(1, line + 1):
        if step < line:
            below, above = place >= step, place + step < line
            for here, z, forward, target in (
                (below, place - step, place < line - 1, up),
                (above, place + step, place > 0, down),
            ):
                q = index_of(z, side, core)

                @pl.when(here)
                def _(q=q):
                    arrived(q)

                pass_on(q, here, forward, target)
        if step == 1:
            relay(across, always)
        else:
            relay(index_of(place - step + 1, 1 - side, core), place >= step - 1)
            relay(index_of(place + step - 1, 1 - side, core), place + step - 1 < line)
    for z in range(line):
        for s in range(2):
            arrived(index_of(z, s, 1 - core))
    for index, (condition, q, target) in enumerate(sends):

        @pl.when(condition)
        def _(index=index, q=q, target=target):
            copy(q, target, index).wait_send()


def gather_clusters(packed, left_sketch, owners):
    line = owners // 4
    cl_dev, width, panels = left_sketch.shape
    shape = (owners * packed.shape[0],) + packed.shape[1:]
    most = 4 + 3 * 2 * (line - 1) + 1 + 2 * (line - 1)
    return pl.pallas_call(
        functools.partial(gather_kernel, line),
        out_shape=(
            jax.ShapeDtypeStruct(shape, packed.dtype),
            jax.ShapeDtypeStruct((cl_dev, 2 * panels, 96), jnp.bfloat16),
            jax.ShapeDtypeStruct((cl_dev, 2 * width, 2 * panels), jnp.bfloat16),
        ),
        in_specs=[pl.BlockSpec(memory_space=pltpu.VMEM)] * 2,
        out_specs=[pl.BlockSpec(memory_space=pltpu.VMEM)] * 3,
        scratch_shapes=[
            pltpu.SemaphoreType.DMA((most,)),
            pltpu.SemaphoreType.DMA((owners,)),
            pltpu.SemaphoreType.DMA,
        ],
        compiler_params=pltpu.CompilerParams(
            collective_id=0, has_side_effects=True, vmem_limit_bytes=vmem_budget
        ),
        name="gather_clusters",
    )(packed, left_sketch)


def scatter_kernel(
    line, x_ref, out_ref, core_buf, side_buf, low_buf, high_buf, send_sem, core_sem, side_sem, low_sem, high_sem
):
    me, core, side, place = neighbours(line)
    size = out_ref.shape[0]

    def block(q):
        return x_ref.at[pl.ds(pl.multiple_of(q * size, size), size)]

    half = place // 2
    order = [3 - 3 * half, 2 - half, 1 - place + 4 * half, place]

    def to_sibling(z, s, index):
        return pltpu.make_async_remote_copy(
            src_ref=block(index_of(z, s, 1 - core)),
            dst_ref=core_buf.at[z * 2 + s],
            send_sem=send_sem.at[index],
            recv_sem=core_sem.at[z * 2 + s],
            device_id={"clus": index_of(place, side, 1 - core)},
        )

    def to_side(z, index):
        return pltpu.make_async_remote_copy(
            src_ref=core_buf.at[z * 2 + 1 - side],
            dst_ref=side_buf.at[z],
            send_sem=send_sem.at[index],
            recv_sem=side_sem.at[z],
            device_id={"clus": index_of(place, 1 - side, core)},
        )

    def along(z, index, buf, sem, target):
        return pltpu.make_async_remote_copy(
            src_ref=side_buf.at[z],
            dst_ref=buf.at[z],
            send_sem=send_sem.at[index],
            recv_sem=sem.at[z],
            device_id={"clus": index_of(target, side, core)},
        )

    def upward(z, index):
        return along(z, index, low_buf, low_sem, place + 1)

    def downward(z, index):
        return along(z, index, high_buf, high_sem, place - 1)

    greet(line, place, side, core)
    for k, z in enumerate(order):
        for j, s in enumerate((1 - side, side)):
            to_sibling(z, s, 2 * k + j).start()
    for k, z in enumerate(order):
        s = 1 - side
        to_sibling(z, s, 2 * k).wait_recv()
        core_buf[z * 2 + s] = core_buf[z * 2 + s] + block(index_of(z, s, core))[...]
        to_side(z, 8 + k).start()
    for k, z in enumerate(order):
        to_sibling(z, side, 2 * k + 1).wait_recv()
        core_buf[z * 2 + side] = core_buf[z * 2 + side] + block(index_of(z, side, core))[...]
    for k, z in enumerate(order):
        to_side(z, 8 + k).wait_recv()
        side_buf[z] = side_buf[z] + core_buf[z * 2 + side]
        if k < line - 1:

            @pl.when((z > place) & (place > 0))
            def _(z=z):
                upward(z, 0).wait_recv()
                side_buf[z] = side_buf[z] + low_buf[z]

            @pl.when((z < place) & (place < line - 1))
            def _(z=z):
                downward(z, 0).wait_recv()
                side_buf[z] = side_buf[z] + high_buf[z]

            @pl.when(z > place)
            def _(z=z, k=k):
                upward(z, 12 + k).start()

            @pl.when(z < place)
            def _(z=z, k=k):
                downward(z, 12 + k).start()

    out_ref[...] = side_buf[place]

    @pl.when(place > 0)
    def _():
        upward(place, 0).wait_recv()
        out_ref[...] = out_ref[...] + low_buf[place]

    @pl.when(place < line - 1)
    def _():
        downward(place, 0).wait_recv()
        out_ref[...] = out_ref[...] + high_buf[place]

    for k, z in enumerate(order):
        for j, s in enumerate((1 - side, side)):
            to_sibling(z, s, 2 * k + j).wait_send()
        to_side(z, 8 + k).wait_send()
        if k < line - 1:

            @pl.when(z > place)
            def _(z=z, k=k):
                upward(z, 12 + k).wait_send()

            @pl.when(z < place)
            def _(z=z, k=k):
                downward(z, 12 + k).wait_send()


def scatter_sums(outgoing, owners):
    line = owners // 4
    clusters, width, panels = outgoing.shape
    block = (clusters // owners, width, panels)
    return pl.pallas_call(
        functools.partial(scatter_kernel, line),
        out_shape=jax.ShapeDtypeStruct(block, outgoing.dtype),
        in_specs=[pl.BlockSpec(memory_space=pltpu.VMEM)],
        out_specs=pl.BlockSpec(memory_space=pltpu.VMEM),
        scratch_shapes=[
            pltpu.VMEM((2 * line,) + block, jnp.float32),
            pltpu.VMEM((line,) + block, jnp.float32),
            pltpu.VMEM((line,) + block, jnp.float32),
            pltpu.VMEM((line,) + block, jnp.float32),
            pltpu.SemaphoreType.DMA((4 * line,)),
            pltpu.SemaphoreType.DMA((2 * line,)),
            pltpu.SemaphoreType.DMA((line,)),
            pltpu.SemaphoreType.DMA((line,)),
            pltpu.SemaphoreType.DMA((line,)),
        ],
        compiler_params=pltpu.CompilerParams(
            collective_id=1, has_side_effects=True, vmem_limit_bytes=vmem_budget
        ),
        name="scatter_sums",
    )(outgoing)


def gather_shards(
    point_offsets,
    panel_normals,
    right_sketch,
    left_sketch,
    pair_count,
    pair_rows,
    pair_offset,
    pair_cols,
):
    owners = lax.axis_size("clus")
    position = lax.axis_index("clus")
    cl_dev, width, panels = right_sketch.shape
    spare = jnp.zeros((cl_dev, geometry_rows - 6, panels), jnp.float32)
    packed = jnp.concatenate([right_sketch, point_offsets, panel_normals, spare], axis=1)
    columns, features, left = gather_clusters(packed, left_sketch, owners)
    target = (position + 1 + pair_offset[:, 0]) % owners
    row_sum, outgoing = sketch_pairs(
        pair_count,
        pair_rows,
        position * cl_dev + pair_rows,
        target * cl_dev + pair_cols,
        features,
        left,
        columns,
        width,
    )
    col_sum = scatter_sums(outgoing, owners)
    return (row_sum, col_sum)


def shards(
    point_offsets,
    panel_normals,
    right_sketch,
    left_sketch,
    pair_count,
    pair_rows,
    pair_offset,
    pair_cols,
):
    cl_dev, width, panels = right_sketch.shape
    held = lax.axis_size("clus") * cl_dev * (2 * width + geometry_rows) * panels * 4
    fits = lax.axis_size("clus") == 16 and held + 2**23 <= vmem_budget
    plan = gather_shards if fits else exchange_shards
    return plan(
        point_offsets,
        panel_normals,
        right_sketch,
        left_sketch,
        pair_count,
        pair_rows,
        pair_offset,
        pair_cols,
    )


def solution(mesh):
    return jax.shard_map(
        shards,
        mesh=mesh,
        in_specs=(
            P(("groups", "clus"), None, None),
            P(("groups", "clus"), None, None),
            P(("groups", "clus"), None, None),
            P(("groups", "clus"), None, None),
            P(("groups", "clus")),
            P(("groups", "clus")),
            P(("groups", "clus"), None),
            P(("groups", "clus")),
        ),
        out_specs=(P(("groups", "clus"), None, None), P(("groups", "clus"), None, None)),
        check_vma=False,
    )
```

```python
import functools
import math

import jax
import jax.numpy as jnp
import numpy as np
from jax import lax
from jax.experimental import pallas as pl
from jax.experimental.pallas import tpu as pltpu
from jax.sharding import PartitionSpec as P

wave_number = 8.0
precise = lax.Precision.HIGHEST


def centers_of(cluster_ids):
    return jnp.stack([cluster_ids % 16, cluster_ids // 16 % 8, cluster_ids // 128], axis=1).astype(
        jnp.float32
    )


def kernel_block(row_pts, row_nrm, col_pts, col_nrm):
    separation = row_pts[:, :, :, None] - col_pts[:, :, None, :]
    distance = jnp.sqrt(jnp.sum(separation * separation, axis=1))
    inverse = 1.0 / distance
    along_row = jnp.sum(separation * row_nrm[:, :, :, None], axis=1)
    along_col = jnp.sum(separation * col_nrm[:, :, None, :], axis=1)
    normal_dot = jnp.sum(row_nrm[:, :, :, None] * col_nrm[:, :, None, :], axis=1)
    green_value = inverse / (4.0 * math.pi)
    cosine = jnp.cos(wave_number * distance)
    sine_part = jnp.sin(wave_number * distance)
    slope_real = green_value * (-cosine * inverse - wave_number * sine_part)
    slope_imag = green_value * (-sine_part * inverse + wave_number * cosine)
    double_real = -along_col * inverse * slope_real
    double_imag = -along_col * inverse * slope_imag
    curve_real = 3.0 * inverse * inverse - wave_number * wave_number
    curve_imag = -3.0 * wave_number * inverse
    second_real = green_value * (cosine * curve_real - sine_part * curve_imag)
    second_imag = green_value * (sine_part * curve_real + cosine * curve_imag)
    tangle = along_row * along_col * inverse * inverse
    hyper_real = -(tangle * second_real + normal_dot * inverse * slope_real)
    hyper_imag = -(tangle * second_imag + normal_dot * inverse * slope_imag)
    return (double_real - hyper_imag / wave_number, double_imag + hyper_real / wave_number)


def sketch_pair(kern_real, kern_imag, right_block, left_block):
    halves = right_block.shape[1] // 2
    real_right = jnp.einsum("bak,bik->bai", right_block, kern_real, precision=precise)
    imag_right = jnp.einsum("bak,bik->bai", right_block, kern_imag, precision=precise)
    row_part = jnp.concatenate(
        [
            real_right[:, :halves] - imag_right[:, halves:],
            imag_right[:, :halves] + real_right[:, halves:],
        ],
        axis=1,
    )
    real_left = jnp.einsum("bai,bik->bak", left_block, kern_real, precision=precise)
    imag_left = jnp.einsum("bai,bik->bak", left_block, kern_imag, precision=precise)
    col_part = jnp.concatenate(
        [
            real_left[:, :halves] + imag_left[:, halves:],
            real_left[:, halves:] - imag_left[:, :halves],
        ],
        axis=1,
    )
    return (row_part, col_part)


def exchange_shards(
    point_offsets,
    panel_normals,
    right_sketch,
    left_sketch,
    pair_count,
    pair_rows,
    pair_offset,
    pair_cols,
):
    owners = lax.axis_size("clus")
    position = lax.axis_index("clus")
    cl_dev, width, panels = right_sketch.shape
    slots = pair_rows.shape[0]
    per_peer = max(2, 2 * slots // owners)
    slot_total = owners * per_peer
    local_ids = position * cl_dev + jnp.arange(cl_dev, dtype=jnp.int32)
    cluster_range = jnp.arange(cl_dev, dtype=jnp.int32)
    points = point_offsets + centers_of(local_ids)[:, :, None]
    live_count = pair_count[0]
    slot_index = jnp.arange(slots, dtype=jnp.int32)
    is_live = slot_index < live_count
    target = (position + 1 + pair_offset[:, 0]) % owners
    peer_hits = (target[:, None] == jnp.arange(owners, dtype=jnp.int32)[None, :]).astype(jnp.int32)
    peer_rank = jnp.sum(jnp.cumsum(peer_hits, axis=0) * peer_hits, axis=1) - 1
    send_pos = target * per_peer + peer_rank
    col_global = target * cl_dev + pair_cols
    zero_buffer = jnp.zeros((slot_total, width, panels), jnp.float32)
    zero_local = jnp.zeros((cl_dev, width, panels), jnp.float32)
    col_tags = (
        jnp.full((slot_total,), -1, jnp.int32).at[send_pos].set(jnp.where(is_live, pair_cols, -1))
    )
    incoming = lax.all_to_all(
        col_tags.reshape(owners, per_peer), "clus", split_axis=0, concat_axis=0, tiled=True
    ).reshape(slot_total)
    picked = jnp.maximum(incoming, 0)
    got_pts, got_nrm, got_right = (
        lax.all_to_all(
            point_offsets[picked].reshape(owners, per_peer, 3, panels),
            "clus",
            split_axis=0,
            concat_axis=0,
            tiled=True,
        ),
        lax.all_to_all(
            panel_normals[picked].reshape(owners, per_peer, 3, panels),
            "clus",
            split_axis=0,
            concat_axis=0,
            tiled=True,
        ),
        lax.all_to_all(
            right_sketch[picked].reshape(owners, per_peer, width, panels),
            "clus",
            split_axis=0,
            concat_axis=0,
            tiled=True,
        ),
    )
    got_pts = got_pts.reshape(slot_total, 3, panels)
    got_nrm = got_nrm.reshape(slot_total, 3, panels)
    got_right = got_right.reshape(slot_total, width, panels)

    def owner_step(block_turn, running):
        row_sum, outgoing = running
        block_index = block_turn * 8 + jnp.arange(8, dtype=jnp.int32)
        weight = (block_index < live_count).astype(jnp.float32)
        slot_at = lax.dynamic_slice_in_dim(send_pos, block_turn * 8, 8)
        row_local = lax.dynamic_slice_in_dim(pair_rows, block_turn * 8, 8)
        col_block = lax.dynamic_slice_in_dim(col_global, block_turn * 8, 8)
        col_pts = got_pts[slot_at] + centers_of(col_block)[:, :, None]
        kern_real, kern_imag = kernel_block(
            points[row_local], panel_normals[row_local], col_pts, got_nrm[slot_at]
        )
        row_part, col_part = sketch_pair(
            kern_real, kern_imag, got_right[slot_at], left_sketch[row_local]
        )
        select = (row_local[:, None] == cluster_range[None, :]).astype(jnp.float32) * weight[
            :, None
        ]
        row_sum = row_sum + jnp.einsum("bl,bak->lak", select, row_part, precision=precise)
        outgoing = outgoing.at[slot_at].add(col_part * weight[:, None, None])
        return (row_sum, outgoing)

    turn_count = (live_count + 7) // 8
    row_sum, outgoing = lax.fori_loop(0, turn_count, owner_step, (zero_local, zero_buffer))
    returned = lax.all_to_all(
        outgoing.reshape(owners, per_peer, width, panels),
        "clus",
        split_axis=0,
        concat_axis=0,
        tiled=True,
    ).reshape(slot_total, width, panels)
    select = (incoming[:, None] == cluster_range[None, :]).astype(jnp.float32)
    col_sum = jnp.einsum("sl,sak->lak", select, returned, precision=precise)
    return (row_sum, col_sum)


geometry_rows = 8
unroll = 8
vmem_budget = 40 * 2**20
kernel_scale = wave_number * wave_number / (12.0 * math.pi)


def phase_coefficients():
    def fit(function, degree):
        series = np.polynomial.chebyshev.Chebyshev.interpolate(function, degree, domain=[0.0, 0.25])
        return [float(c) for c in series.convert(kind=np.polynomial.Polynomial).coef]

    def sine_ratio(z):
        return math.sqrt(2.0) * math.pi * np.sinc(np.sqrt(z))

    def cosine(z):
        return math.sqrt(2.0) * np.cos(math.pi * np.sqrt(z))

    return fit(sine_ratio, 3), fit(cosine, 4)


sine_terms, cosine_terms = phase_coefficients()


def horner(terms, z):
    value = terms[-1] * z + terms[-2]
    for term in terms[-3::-1]:
        value = value * z + term
    return value


def split_two(x):
    high = x.astype(jnp.bfloat16)
    return high, (x - high.astype(jnp.float32)).astype(jnp.bfloat16)


def rounded(x):
    return x.astype(jnp.bfloat16).astype(jnp.float32)


def row_features(geometry):
    index = lax.broadcasted_iota(jnp.int32, geometry.shape, 0)
    x = [wave_number * geometry[i : i + 1] for i in range(3)]
    n = [geometry[i : i + 1] for i in range(3, 6)]
    zero = jnp.zeros_like(x[0])
    one = zero + 1.0

    def rows(parts):
        block = jnp.zeros_like(geometry)
        for i, part in parts.items():
            block = jnp.where(index == i, part, block)
        return block

    def form(parts, constant):
        block = rows(parts)
        high = rounded(block)
        low = block - high
        c_high = rounded(constant)
        c_middle = rounded(constant - c_high)
        tail = rows({0: c_high, 1: c_middle, 2: constant - c_high - c_middle})
        return jnp.concatenate([high, high, high, low, low, tail], axis=0)

    square = form(
        {0: -2.0 * x[0], 1: -2.0 * x[1], 2: -2.0 * x[2], 6: one},
        x[0] * x[0] + x[1] * x[1] + x[2] * x[2],
    )
    along_col = form({3: x[0], 4: x[1], 5: x[2], 7: -one}, zero)
    along_row = form({0: -n[0], 1: -n[1], 2: -n[2]}, x[0] * n[0] + x[1] * n[1] + x[2] * n[2])
    normal_dot = form({3: n[0], 4: n[1], 5: n[2]}, zero)
    empty = jnp.zeros((32, geometry.shape[1]), jnp.float32)
    left = jnp.concatenate([square, along_col, empty], axis=0)
    right = jnp.concatenate([along_row, normal_dot, empty], axis=0)
    both = jnp.concatenate([left.T, right.T], axis=0)
    return both[:, :96].astype(jnp.bfloat16)


def left_operand(left):
    halves = left.shape[0] // 2

    def complex_rows(block):
        real, imag = block[:halves], block[halves:]
        return [jnp.concatenate([real, imag], axis=1), jnp.concatenate([imag, -real], axis=1)]

    high, low = split_two(left)
    return jnp.concatenate(complex_rows(high) + complex_rows(low), axis=0)


def pair_parts(features, left, column, width, shift):
    panels = column.shape[1]
    halves = width // 2
    geometry = column[width:]
    index = lax.broadcasted_iota(jnp.int32, geometry.shape, 0)
    move = jnp.where(
        index == 0, shift[0], jnp.where(index == 1, shift[1], jnp.where(index == 2, shift[2], 0.0))
    )
    base = jnp.where(index < 3, wave_number, 1.0) * (geometry + move)
    y = [base[i : i + 1] for i in range(3)]
    m = [base[i : i + 1] for i in range(3, 6)]
    square = y[0] * y[0] + y[1] * y[1] + y[2] * y[2]
    inner = y[0] * m[0] + y[1] * m[1] + y[2] * m[2]
    full = jnp.where(index == 6, square, jnp.where(index == 7, inner, base))
    high = full.astype(jnp.bfloat16).astype(jnp.float32)
    rest = full - high
    middle = rest.astype(jnp.bfloat16).astype(jnp.float32)
    low = rest - middle
    stack = jnp.concatenate([high, middle, low, high, middle, jnp.ones_like(high)], axis=0).astype(
        jnp.bfloat16
    )
    empty = jnp.zeros_like(stack)
    operand = jnp.concatenate(
        [jnp.concatenate([stack, empty], axis=1), jnp.concatenate([empty, stack], axis=1)], axis=0
    )
    forms = jnp.dot(features, operand, preferred_element_type=jnp.float32)

    pieces = []
    chunk = 32
    magic = 1.5 * 2.0**23
    for start in range(0, panels, chunk):
        r2 = forms[start : start + chunk, :panels]
        along_col = forms[start : start + chunk, panels:]
        along_row = forms[panels + start : panels + start + chunk, :panels]
        normal_dot = forms[panels + start : panels + start + chunk, panels:]
        inverse = lax.rsqrt(r2)
        turns = (r2 * inverse) * (0.5 / math.pi)
        turns = turns - ((turns + magic) - magic)
        z = turns * turns
        sine_half = turns * horner(sine_terms, z)
        cosine_half = horner(cosine_terms, z)
        weight = 3.0 * (inverse * inverse)
        scaled = sine_half * weight
        sine_w = scaled * cosine_half
        cosine_w = weight - scaled * sine_half
        both = along_col * along_row
        inner_term = normal_dot - both * weight
        real = inner_term + along_col * inverse
        imag = inverse * (inner_term + both) - along_col
        pieces.append((cosine_w * real - sine_w * imag, cosine_w * imag + sine_w * real))
    real, imag = [jnp.concatenate([piece[q] for piece in pieces], axis=0) for q in range(2)]

    def operand_of(real, imag):
        return jnp.concatenate(
            [jnp.concatenate(split_two(real), axis=1), jnp.concatenate(split_two(imag), axis=1)],
            axis=0,
        )

    w_high, w_low = split_two(column[:width])

    def complex_rows(block):
        real, imag = block[:halves], block[halves:]
        return [jnp.concatenate([real, -imag], axis=1), jnp.concatenate([imag, real], axis=1)]

    right = jnp.concatenate(complex_rows(w_high) + complex_rows(w_low), axis=0)
    row_out = jnp.dot(right, operand_of(real.T, imag.T), preferred_element_type=jnp.float32)
    col_out = jnp.dot(left, operand_of(real, imag), preferred_element_type=jnp.float32)

    def fold(out):
        return (
            out[:width, :panels]
            + out[:width, panels:]
            + (out[width:, :panels] + out[width:, panels:])
        )

    return fold(row_out), fold(col_out)


def pair_kernel(
    live_ref, row_ref, global_row_ref, col_ref, features_ref, left_ref, column_ref, row_out, col_out
):
    row_out[...] = jnp.zeros_like(row_out)
    width = row_out.shape[1]

    def clear(i, carry):
        col_out[i] = jnp.zeros(col_out.shape[1:], jnp.float32)
        return carry

    lax.fori_loop(0, col_out.shape[0], clear, 0)
    live = live_ref[0]

    def center(c):
        return (c & 15, (c >> 4) & 7, c >> 7)

    def turn(step, carry):
        done = []
        for k in range(unroll):
            slot = step * unroll + k
            row = row_ref[slot]
            col = col_ref[slot]
            shift = [
                (b - a).astype(jnp.float32)
                for a, b in zip(center(global_row_ref[slot]), center(col))
            ]
            parts = pair_parts(features_ref[row], left_ref[row], column_ref[col], width, shift)
            scale = jnp.where(slot < live, kernel_scale, 0.0)
            done.append((row, col, parts[0] * scale, parts[1] * scale))
        for row, col, row_part, col_part in done:
            row_out[row] += row_part
            col_out[col] += col_part
        return carry

    lax.fori_loop(0, (live + unroll - 1) // unroll, turn, 0)


def sketch_pairs(live, rows, global_rows, cols, features, left, columns, width):
    cl_dev = features.shape[0]
    clusters, _, panels = columns.shape
    return pl.pallas_call(
        pair_kernel,
        grid_spec=pltpu.PrefetchScalarGridSpec(
            num_scalar_prefetch=4,
            in_specs=[pl.BlockSpec(memory_space=pltpu.VMEM)] * 3,
            out_specs=[pl.BlockSpec(memory_space=pltpu.VMEM)] * 2,
        ),
        out_shape=(
            jax.ShapeDtypeStruct((cl_dev, width, panels), jnp.float32),
            jax.ShapeDtypeStruct((clusters, width, panels), jnp.float32),
        ),
        compiler_params=pltpu.CompilerParams(vmem_limit_bytes=vmem_budget),
        name="pair_sketches",
    )(live, rows, global_rows, cols, features, left, columns)


def neighbours(line):
    me = lax.axis_index("clus")
    core, side, place = me % 2, me // 2 % 2, me // 4
    return me, core, side, place


def index_of(place, side, core):
    return place * 4 + side * 2 + core


def greet(line, place, side, core):
    barrier = pltpu.get_barrier_semaphore()

    def call(target):
        pl.semaphore_signal(barrier, inc=1, device_id={"clus": target})

    call(index_of(place, side, 1 - core))
    call(index_of(place, 1 - side, core))

    @pl.when(place > 0)
    def _():
        call(index_of(place - 1, side, core))

    @pl.when(place < line - 1)
    def _():
        call(index_of(place + 1, side, core))

    pl.semaphore_wait(barrier, 2 + jnp.minimum(place, 1) + jnp.minimum(line - 1 - place, 1))


def gather_kernel(
    line,
    x_ref,
    sketch_ref,
    out_ref,
    features_ref,
    left_ref,
    send_sem,
    recv_sem,
    local_sem,
):
    me, core, side, place = neighbours(line)
    size = x_ref.shape[0]

    def block(q):
        return out_ref.at[pl.ds(pl.multiple_of(q * size, size), size)]

    def copy(q, target, index):
        return pltpu.make_async_remote_copy(
            src_ref=block(q),
            dst_ref=block(q),
            send_sem=send_sem.at[index],
            recv_sem=recv_sem.at[q],
            device_id={"clus": target},
        )

    def arrived(q):
        copy(q, index_of(place, side, 1 - core), 0).wait_recv()

    mine = pltpu.make_async_copy(x_ref, block(me), local_sem)
    mine.start()
    greet(line, place, side, core)
    mine.wait()

    sends = []

    def send(condition, q, target):
        sends.append((condition, q, target))
        index = len(sends) - 1

        @pl.when(condition)
        def _():
            copy(q, target, index).start()

    always = place >= 0
    sibling = index_of(place, side, 1 - core)
    across = index_of(place, 1 - side, core)
    down = index_of(place - 1, side, core)
    up = index_of(place + 1, side, core)

    def pass_on(q, here, forward, target):
        send(here & forward, q, target)
        send(here, q, across)
        send(here, q, sibling)

    def relay(q, here):
        @pl.when(here)
        def _():
            arrived(q)

        send(here, q, sibling)

    send(place < line - 1, me, up)
    send(place > 0, me, down)
    send(always, me, across)
    send(always, me, sibling)
    width = sketch_ref.shape[1]

    def prepare(i, carry):
        features_ref[i] = row_features(x_ref[i][width:])
        left_ref[i] = left_operand(sketch_ref[i])
        return carry

    lax.fori_loop(0, size, prepare, 0)
    for step in range(1, line + 1):
        if step < line:
            below, above = place >= step, place + step < line
            for here, z, forward, target in (
                (below, place - step, place < line - 1, up),
                (above, place + step, place > 0, down),
            ):
                q = index_of(z, side, core)

                @pl.when(here)
                def _(q=q):
                    arrived(q)

                pass_on(q, here, forward, target)
        if step == 1:
            relay(across, always)
        else:
            relay(index_of(place - step + 1, 1 - side, core), place >= step - 1)
            relay(index_of(place + step - 1, 1 - side, core), place + step - 1 < line)
    for z in range(line):
        for s in range(2):
            arrived(index_of(z, s, 1 - core))
    for index, (condition, q, target) in enumerate(sends):

        @pl.when(condition)
        def _(index=index, q=q, target=target):
            copy(q, target, index).wait_send()


def gather_clusters(packed, left_sketch, owners):
    line = owners // 4
    cl_dev, width, panels = left_sketch.shape
    shape = (owners * packed.shape[0],) + packed.shape[1:]
    most = 4 + 3 * 2 * (line - 1) + 1 + 2 * (line - 1)
    return pl.pallas_call(
        functools.partial(gather_kernel, line),
        out_shape=(
            jax.ShapeDtypeStruct(shape, packed.dtype),
            jax.ShapeDtypeStruct((cl_dev, 2 * panels, 96), jnp.bfloat16),
            jax.ShapeDtypeStruct((cl_dev, 2 * width, 2 * panels), jnp.bfloat16),
        ),
        in_specs=[pl.BlockSpec(memory_space=pltpu.VMEM)] * 2,
        out_specs=[pl.BlockSpec(memory_space=pltpu.VMEM)] * 3,
        scratch_shapes=[
            pltpu.SemaphoreType.DMA((most,)),
            pltpu.SemaphoreType.DMA((owners,)),
            pltpu.SemaphoreType.DMA,
        ],
        compiler_params=pltpu.CompilerParams(
            collective_id=0, has_side_effects=True, vmem_limit_bytes=vmem_budget
        ),
        name="gather_clusters",
    )(packed, left_sketch)


def scatter_kernel(
    line, x_ref, out_ref, core_buf, side_buf, low_buf, high_buf, send_sem, core_sem, side_sem, low_sem, high_sem
):
    me, core, side, place = neighbours(line)
    size = out_ref.shape[0]

    def block(q):
        return x_ref.at[pl.ds(pl.multiple_of(q * size, size), size)]

    half = place // 2
    order = [3 - 3 * half, 2 - half, 1 - place + 4 * half, place]

    def to_sibling(z, s, index):
        return pltpu.make_async_remote_copy(
            src_ref=block(index_of(z, s, 1 - core)),
            dst_ref=core_buf.at[z * 2 + s],
            send_sem=send_sem.at[index],
            recv_sem=core_sem.at[z * 2 + s],
            device_id={"clus": index_of(place, side, 1 - core)},
        )

    def to_side(z, index):
        return pltpu.make_async_remote_copy(
            src_ref=core_buf.at[z * 2 + 1 - side],
            dst_ref=side_buf.at[z],
            send_sem=send_sem.at[index],
            recv_sem=side_sem.at[z],
            device_id={"clus": index_of(place, 1 - side, core)},
        )

    def along(z, index, buf, sem, target):
        return pltpu.make_async_remote_copy(
            src_ref=side_buf.at[z],
            dst_ref=buf.at[z],
            send_sem=send_sem.at[index],
            recv_sem=sem.at[z],
            device_id={"clus": index_of(target, side, core)},
        )

    def upward(z, index):
        return along(z, index, low_buf, low_sem, place + 1)

    def downward(z, index):
        return along(z, index, high_buf, high_sem, place - 1)

    greet(line, place, side, core)
    for k, z in enumerate(order):
        for j, s in enumerate((1 - side, side)):
            to_sibling(z, s, 2 * k + j).start()
    for k, z in enumerate(order):
        s = 1 - side
        to_sibling(z, s, 2 * k).wait_recv()
        core_buf[z * 2 + s] = core_buf[z * 2 + s] + block(index_of(z, s, core))[...]
        to_side(z, 8 + k).start()
    for k, z in enumerate(order):
        to_sibling(z, side, 2 * k + 1).wait_recv()
        core_buf[z * 2 + side] = core_buf[z * 2 + side] + block(index_of(z, side, core))[...]
    for k, z in enumerate(order):
        to_side(z, 8 + k).wait_recv()
        side_buf[z] = side_buf[z] + core_buf[z * 2 + side]
        if k < line - 1:

            @pl.when((z > place) & (place > 0))
            def _(z=z):
                upward(z, 0).wait_recv()
                side_buf[z] = side_buf[z] + low_buf[z]

            @pl.when((z < place) & (place < line - 1))
            def _(z=z):
                downward(z, 0).wait_recv()
                side_buf[z] = side_buf[z] + high_buf[z]

            @pl.when(z > place)
            def _(z=z, k=k):
                upward(z, 12 + k).start()

            @pl.when(z < place)
            def _(z=z, k=k):
                downward(z, 12 + k).start()

    out_ref[...] = side_buf[place]

    @pl.when(place > 0)
    def _():
        upward(place, 0).wait_recv()
        out_ref[...] = out_ref[...] + low_buf[place]

    @pl.when(place < line - 1)
    def _():
        downward(place, 0).wait_recv()
        out_ref[...] = out_ref[...] + high_buf[place]

    for k, z in enumerate(order):
        for j, s in enumerate((1 - side, side)):
            to_sibling(z, s, 2 * k + j).wait_send()
        to_side(z, 8 + k).wait_send()
        if k < line - 1:

            @pl.when(z > place)
            def _(z=z, k=k):
                upward(z, 12 + k).wait_send()

            @pl.when(z < place)
            def _(z=z, k=k):
                downward(z, 12 + k).wait_send()


def scatter_sums(outgoing, owners):
    line = owners // 4
    clusters, width, panels = outgoing.shape
    block = (clusters // owners, width, panels)
    return pl.pallas_call(
        functools.partial(scatter_kernel, line),
        out_shape=jax.ShapeDtypeStruct(block, outgoing.dtype),
        in_specs=[pl.BlockSpec(memory_space=pltpu.VMEM)],
        out_specs=pl.BlockSpec(memory_space=pltpu.VMEM),
        scratch_shapes=[
            pltpu.VMEM((2 * line,) + block, jnp.float32),
            pltpu.VMEM((line,) + block, jnp.float32),
            pltpu.VMEM((line,) + block, jnp.float32),
            pltpu.VMEM((line,) + block, jnp.float32),
            pltpu.SemaphoreType.DMA((4 * line,)),
            pltpu.SemaphoreType.DMA((2 * line,)),
            pltpu.SemaphoreType.DMA((line,)),
            pltpu.SemaphoreType.DMA((line,)),
            pltpu.SemaphoreType.DMA((line,)),
        ],
        compiler_params=pltpu.CompilerParams(
            collective_id=1, has_side_effects=True, vmem_limit_bytes=vmem_budget
        ),
        name="scatter_sums",
    )(outgoing)


def gather_shards(
    point_offsets,
    panel_normals,
    right_sketch,
    left_sketch,
    pair_count,
    pair_rows,
    pair_offset,
    pair_cols,
):
    owners = lax.axis_size("clus")
    position = lax.axis_index("clus")
    cl_dev, width, panels = right_sketch.shape
    spare = jnp.zeros((cl_dev, geometry_rows - 6, panels), jnp.float32)
    packed = jnp.concatenate([right_sketch, point_offsets, panel_normals, spare], axis=1)
    columns, features, left = gather_clusters(packed, left_sketch, owners)
    target = (position + 1 + pair_offset[:, 0]) % owners
    row_sum, outgoing = sketch_pairs(
        pair_count,
        pair_rows,
        position * cl_dev + pair_rows,
        target * cl_dev + pair_cols,
        features,
        left,
        columns,
        width,
    )
    col_sum = scatter_sums(outgoing, owners)
    return (row_sum, col_sum)


def shards(
    point_offsets,
    panel_normals,
    right_sketch,
    left_sketch,
    pair_count,
    pair_rows,
    pair_offset,
    pair_cols,
):
    cl_dev, width, panels = right_sketch.shape
    held = lax.axis_size("clus") * cl_dev * (2 * width + geometry_rows) * panels * 4
    fits = lax.axis_size("clus") == 16 and held + 2**23 <= vmem_budget
    plan = gather_shards if fits else exchange_shards
    return plan(
        point_offsets,
        panel_normals,
        right_sketch,
        left_sketch,
        pair_count,
        pair_rows,
        pair_offset,
        pair_cols,
    )


def solution(mesh):
    return jax.shard_map(
        shards,
        mesh=mesh,
        in_specs=(
            P(("groups", "clus"), None, None),
            P(("groups", "clus"), None, None),
            P(("groups", "clus"), None, None),
            P(("groups", "clus"), None, None),
            P(("groups", "clus")),
            P(("groups", "clus")),
            P(("groups", "clus"), None),
            P(("groups", "clus")),
        ),
        out_specs=(P(("groups", "clus"), None, None), P(("groups", "clus"), None, None)),
        check_vma=False,
    )
```

```python
import functools
import math

import jax
import jax.numpy as jnp
import numpy as np
from jax import lax
from jax.experimental import pallas as pl
from jax.experimental.pallas import tpu as pltpu
from jax.sharding import PartitionSpec as P

wave_number = 8.0
precise = lax.Precision.HIGHEST


def centers_of(cluster_ids):
    return jnp.stack([cluster_ids % 16, cluster_ids // 16 % 8, cluster_ids // 128], axis=1).astype(
        jnp.float32
    )


def kernel_block(row_pts, row_nrm, col_pts, col_nrm):
    separation = row_pts[:, :, :, None] - col_pts[:, :, None, :]
    distance = jnp.sqrt(jnp.sum(separation * separation, axis=1))
    inverse = 1.0 / distance
    along_row = jnp.sum(separation * row_nrm[:, :, :, None], axis=1)
    along_col = jnp.sum(separation * col_nrm[:, :, None, :], axis=1)
    normal_dot = jnp.sum(row_nrm[:, :, :, None] * col_nrm[:, :, None, :], axis=1)
    green_value = inverse / (4.0 * math.pi)
    cosine = jnp.cos(wave_number * distance)
    sine_part = jnp.sin(wave_number * distance)
    slope_real = green_value * (-cosine * inverse - wave_number * sine_part)
    slope_imag = green_value * (-sine_part * inverse + wave_number * cosine)
    double_real = -along_col * inverse * slope_real
    double_imag = -along_col * inverse * slope_imag
    curve_real = 3.0 * inverse * inverse - wave_number * wave_number
    curve_imag = -3.0 * wave_number * inverse
    second_real = green_value * (cosine * curve_real - sine_part * curve_imag)
    second_imag = green_value * (sine_part * curve_real + cosine * curve_imag)
    tangle = along_row * along_col * inverse * inverse
    hyper_real = -(tangle * second_real + normal_dot * inverse * slope_real)
    hyper_imag = -(tangle * second_imag + normal_dot * inverse * slope_imag)
    return (double_real - hyper_imag / wave_number, double_imag + hyper_real / wave_number)


def sketch_pair(kern_real, kern_imag, right_block, left_block):
    halves = right_block.shape[1] // 2
    real_right = jnp.einsum("bak,bik->bai", right_block, kern_real, precision=precise)
    imag_right = jnp.einsum("bak,bik->bai", right_block, kern_imag, precision=precise)
    row_part = jnp.concatenate(
        [
            real_right[:, :halves] - imag_right[:, halves:],
            imag_right[:, :halves] + real_right[:, halves:],
        ],
        axis=1,
    )
    real_left = jnp.einsum("bai,bik->bak", left_block, kern_real, precision=precise)
    imag_left = jnp.einsum("bai,bik->bak", left_block, kern_imag, precision=precise)
    col_part = jnp.concatenate(
        [
            real_left[:, :halves] + imag_left[:, halves:],
            real_left[:, halves:] - imag_left[:, :halves],
        ],
        axis=1,
    )
    return (row_part, col_part)


def exchange_shards(
    point_offsets,
    panel_normals,
    right_sketch,
    left_sketch,
    pair_count,
    pair_rows,
    pair_offset,
    pair_cols,
):
    owners = lax.axis_size("clus")
    position = lax.axis_index("clus")
    cl_dev, width, panels = right_sketch.shape
    slots = pair_rows.shape[0]
    per_peer = max(2, 2 * slots // owners)
    slot_total = owners * per_peer
    local_ids = position * cl_dev + jnp.arange(cl_dev, dtype=jnp.int32)
    cluster_range = jnp.arange(cl_dev, dtype=jnp.int32)
    points = point_offsets + centers_of(local_ids)[:, :, None]
    live_count = pair_count[0]
    slot_index = jnp.arange(slots, dtype=jnp.int32)
    is_live = slot_index < live_count
    target = (position + 1 + pair_offset[:, 0]) % owners
    peer_hits = (target[:, None] == jnp.arange(owners, dtype=jnp.int32)[None, :]).astype(jnp.int32)
    peer_rank = jnp.sum(jnp.cumsum(peer_hits, axis=0) * peer_hits, axis=1) - 1
    send_pos = target * per_peer + peer_rank
    col_global = target * cl_dev + pair_cols
    zero_buffer = jnp.zeros((slot_total, width, panels), jnp.float32)
    zero_local = jnp.zeros((cl_dev, width, panels), jnp.float32)
    col_tags = (
        jnp.full((slot_total,), -1, jnp.int32).at[send_pos].set(jnp.where(is_live, pair_cols, -1))
    )
    incoming = lax.all_to_all(
        col_tags.reshape(owners, per_peer), "clus", split_axis=0, concat_axis=0, tiled=True
    ).reshape(slot_total)
    picked = jnp.maximum(incoming, 0)
    got_pts, got_nrm, got_right = (
        lax.all_to_all(
            point_offsets[picked].reshape(owners, per_peer, 3, panels),
            "clus",
            split_axis=0,
            concat_axis=0,
            tiled=True,
        ),
        lax.all_to_all(
            panel_normals[picked].reshape(owners, per_peer, 3, panels),
            "clus",
            split_axis=0,
            concat_axis=0,
            tiled=True,
        ),
        lax.all_to_all(
            right_sketch[picked].reshape(owners, per_peer, width, panels),
            "clus",
            split_axis=0,
            concat_axis=0,
            tiled=True,
        ),
    )
    got_pts = got_pts.reshape(slot_total, 3, panels)
    got_nrm = got_nrm.reshape(slot_total, 3, panels)
    got_right = got_right.reshape(slot_total, width, panels)

    def owner_step(block_turn, running):
        row_sum, outgoing = running
        block_index = block_turn * 8 + jnp.arange(8, dtype=jnp.int32)
        weight = (block_index < live_count).astype(jnp.float32)
        slot_at = lax.dynamic_slice_in_dim(send_pos, block_turn * 8, 8)
        row_local = lax.dynamic_slice_in_dim(pair_rows, block_turn * 8, 8)
        col_block = lax.dynamic_slice_in_dim(col_global, block_turn * 8, 8)
        col_pts = got_pts[slot_at] + centers_of(col_block)[:, :, None]
        kern_real, kern_imag = kernel_block(
            points[row_local], panel_normals[row_local], col_pts, got_nrm[slot_at]
        )
        row_part, col_part = sketch_pair(
            kern_real, kern_imag, got_right[slot_at], left_sketch[row_local]
        )
        select = (row_local[:, None] == cluster_range[None, :]).astype(jnp.float32) * weight[
            :, None
        ]
        row_sum = row_sum + jnp.einsum("bl,bak->lak", select, row_part, precision=precise)
        outgoing = outgoing.at[slot_at].add(col_part * weight[:, None, None])
        return (row_sum, outgoing)

    turn_count = (live_count + 7) // 8
    row_sum, outgoing = lax.fori_loop(0, turn_count, owner_step, (zero_local, zero_buffer))
    returned = lax.all_to_all(
        outgoing.reshape(owners, per_peer, width, panels),
        "clus",
        split_axis=0,
        concat_axis=0,
        tiled=True,
    ).reshape(slot_total, width, panels)
    select = (incoming[:, None] == cluster_range[None, :]).astype(jnp.float32)
    col_sum = jnp.einsum("sl,sak->lak", select, returned, precision=precise)
    return (row_sum, col_sum)


geometry_rows = 8
unroll = 8
vmem_budget = 40 * 2**20
kernel_scale = wave_number * wave_number / (12.0 * math.pi)


def phase_coefficients():
    def fit(function, degree):
        series = np.polynomial.chebyshev.Chebyshev.interpolate(function, degree, domain=[0.0, 0.25])
        return [float(c) for c in series.convert(kind=np.polynomial.Polynomial).coef]

    def sine_ratio(z):
        return math.sqrt(2.0) * math.pi * np.sinc(np.sqrt(z))

    def cosine(z):
        return math.sqrt(2.0) * np.cos(math.pi * np.sqrt(z))

    return fit(sine_ratio, 3), fit(cosine, 4)


sine_terms, cosine_terms = phase_coefficients()


def horner(terms, z):
    value = terms[-1] * z + terms[-2]
    for term in terms[-3::-1]:
        value = value * z + term
    return value


def split_two(x):
    high = x.astype(jnp.bfloat16)
    return high, (x - high.astype(jnp.float32)).astype(jnp.bfloat16)


def rounded(x):
    return x.astype(jnp.bfloat16).astype(jnp.float32)


def row_features(geometry):
    index = lax.broadcasted_iota(jnp.int32, geometry.shape, 0)
    x = [wave_number * geometry[i : i + 1] for i in range(3)]
    n = [geometry[i : i + 1] for i in range(3, 6)]
    zero = jnp.zeros_like(x[0])
    one = zero + 1.0

    def rows(parts):
        block = jnp.zeros_like(geometry)
        for i, part in parts.items():
            block = jnp.where(index == i, part, block)
        return block

    def form(parts, constant):
        block = rows(parts)
        high = rounded(block)
        low = block - high
        c_high = rounded(constant)
        c_middle = rounded(constant - c_high)
        tail = rows({0: c_high, 1: c_middle, 2: constant - c_high - c_middle})
        return jnp.concatenate([high, high, high, low, low, tail], axis=0)

    square = form(
        {0: -2.0 * x[0], 1: -2.0 * x[1], 2: -2.0 * x[2], 6: one},
        x[0] * x[0] + x[1] * x[1] + x[2] * x[2],
    )
    along_col = form({3: x[0], 4: x[1], 5: x[2], 7: -one}, zero)
    along_row = form({0: -n[0], 1: -n[1], 2: -n[2]}, x[0] * n[0] + x[1] * n[1] + x[2] * n[2])
    normal_dot = form({3: n[0], 4: n[1], 5: n[2]}, zero)
    empty = jnp.zeros((32, geometry.shape[1]), jnp.float32)
    left = jnp.concatenate([square, along_col, empty], axis=0)
    right = jnp.concatenate([along_row, normal_dot, empty], axis=0)
    both = jnp.concatenate([left.T, right.T], axis=0)
    return both[:, :96].astype(jnp.bfloat16)


def left_operand(left):
    halves = left.shape[0] // 2

    def complex_rows(block):
        real, imag = block[:halves], block[halves:]
        return [jnp.concatenate([real, imag], axis=1), jnp.concatenate([imag, -real], axis=1)]

    high, low = split_two(left)
    return jnp.concatenate(complex_rows(high) + complex_rows(low), axis=0)


def pair_parts(features, left, column, width, shift):
    panels = column.shape[1]
    halves = width // 2
    geometry = column[width:]
    index = lax.broadcasted_iota(jnp.int32, geometry.shape, 0)
    move = jnp.where(
        index == 0, shift[0], jnp.where(index == 1, shift[1], jnp.where(index == 2, shift[2], 0.0))
    )
    base = jnp.where(index < 3, wave_number, 1.0) * (geometry + move)
    y = [base[i : i + 1] for i in range(3)]
    m = [base[i : i + 1] for i in range(3, 6)]
    square = y[0] * y[0] + y[1] * y[1] + y[2] * y[2]
    inner = y[0] * m[0] + y[1] * m[1] + y[2] * m[2]
    full = jnp.where(index == 6, square, jnp.where(index == 7, inner, base))
    high = full.astype(jnp.bfloat16).astype(jnp.float32)
    rest = full - high
    middle = rest.astype(jnp.bfloat16).astype(jnp.float32)
    low = rest - middle
    stack = jnp.concatenate([high, middle, low, high, middle, jnp.ones_like(high)], axis=0).astype(
        jnp.bfloat16
    )
    empty = jnp.zeros_like(stack)
    operand = jnp.concatenate(
        [jnp.concatenate([stack, empty], axis=1), jnp.concatenate([empty, stack], axis=1)], axis=0
    )
    forms = jnp.dot(features, operand, preferred_element_type=jnp.float32)

    pieces = []
    chunk = 32
    magic = 1.5 * 2.0**23
    for start in range(0, panels, chunk):
        r2 = forms[start : start + chunk, :panels]
        along_col = forms[start : start + chunk, panels:]
        along_row = forms[panels + start : panels + start + chunk, :panels]
        normal_dot = forms[panels + start : panels + start + chunk, panels:]
        inverse = lax.rsqrt(r2)
        turns = (r2 * inverse) * (0.5 / math.pi)
        turns = turns - ((turns + magic) - magic)
        z = turns * turns
        sine_half = turns * horner(sine_terms, z)
        cosine_half = horner(cosine_terms, z)
        weight = 3.0 * (inverse * inverse)
        scaled = sine_half * weight
        sine_w = scaled * cosine_half
        cosine_w = weight - scaled * sine_half
        both = along_col * along_row
        inner_term = normal_dot - both * weight
        real = inner_term + along_col * inverse
        imag = inverse * (inner_term + both) - along_col
        pieces.append((cosine_w * real - sine_w * imag, cosine_w * imag + sine_w * real))
    real, imag = [jnp.concatenate([piece[q] for piece in pieces], axis=0) for q in range(2)]

    def operand_of(real, imag):
        return jnp.concatenate(
            [jnp.concatenate(split_two(real), axis=1), jnp.concatenate(split_two(imag), axis=1)],
            axis=0,
        )

    w_high, w_low = split_two(column[:width])

    def complex_rows(block):
        real, imag = block[:halves], block[halves:]
        return [jnp.concatenate([real, -imag], axis=1), jnp.concatenate([imag, real], axis=1)]

    right = jnp.concatenate(complex_rows(w_high) + complex_rows(w_low), axis=0)
    row_out = jnp.dot(right, operand_of(real.T, imag.T), preferred_element_type=jnp.float32)
    col_out = jnp.dot(left, operand_of(real, imag), preferred_element_type=jnp.float32)

    def fold(out):
        return (
            out[:width, :panels]
            + out[:width, panels:]
            + (out[width:, :panels] + out[width:, panels:])
        )

    return fold(row_out), fold(col_out)


def pair_kernel(
    live_ref, row_ref, global_row_ref, col_ref, features_ref, left_ref, column_ref, row_out, col_out
):
    row_out[...] = jnp.zeros_like(row_out)
    width = row_out.shape[1]

    def clear(i, carry):
        col_out[i] = jnp.zeros(col_out.shape[1:], jnp.float32)
        return carry

    lax.fori_loop(0, col_out.shape[0], clear, 0)
    live = live_ref[0]

    def center(c):
        return (c & 15, (c >> 4) & 7, c >> 7)

    def turn(step, carry):
        done = []
        for k in range(unroll):
            slot = step * unroll + k
            row = row_ref[slot]
            col = col_ref[slot]
            shift = [
                (b - a).astype(jnp.float32)
                for a, b in zip(center(global_row_ref[slot]), center(col))
            ]
            parts = pair_parts(features_ref[row], left_ref[row], column_ref[col], width, shift)
            scale = jnp.where(slot < live, kernel_scale, 0.0)
            done.append((row, col, parts[0] * scale, parts[1] * scale))
        for row, col, row_part, col_part in done:
            row_out[row] += row_part
            col_out[col] += col_part
        return carry

    lax.fori_loop(0, (live + unroll - 1) // unroll, turn, 0)


def sketch_pairs(live, rows, global_rows, cols, features, left, columns, width):
    cl_dev = features.shape[0]
    clusters, _, panels = columns.shape
    return pl.pallas_call(
        pair_kernel,
        grid_spec=pltpu.PrefetchScalarGridSpec(
            num_scalar_prefetch=4,
            in_specs=[pl.BlockSpec(memory_space=pltpu.VMEM)] * 3,
            out_specs=[pl.BlockSpec(memory_space=pltpu.VMEM)] * 2,
        ),
        out_shape=(
            jax.ShapeDtypeStruct((cl_dev, width, panels), jnp.float32),
            jax.ShapeDtypeStruct((clusters, width, panels), jnp.float32),
        ),
        compiler_params=pltpu.CompilerParams(vmem_limit_bytes=vmem_budget),
        name="pair_sketches",
    )(live, rows, global_rows, cols, features, left, columns)


def neighbours(line):
    me = lax.axis_index("clus")
    core, side, place = me % 2, me // 2 % 2, me // 4
    return me, core, side, place


def index_of(place, side, core):
    return place * 4 + side * 2 + core


def greet(line, place, side, core):
    barrier = pltpu.get_barrier_semaphore()

    def call(target):
        pl.semaphore_signal(barrier, inc=1, device_id={"clus": target})

    call(index_of(place, side, 1 - core))
    call(index_of(place, 1 - side, core))

    @pl.when(place > 0)
    def _():
        call(index_of(place - 1, side, core))

    @pl.when(place < line - 1)
    def _():
        call(index_of(place + 1, side, core))

    pl.semaphore_wait(barrier, 2 + jnp.minimum(place, 1) + jnp.minimum(line - 1 - place, 1))


def gather_kernel(
    line,
    x_ref,
    sketch_ref,
    out_ref,
    features_ref,
    left_ref,
    send_sem,
    recv_sem,
    local_sem,
):
    me, core, side, place = neighbours(line)
    size = x_ref.shape[0]
    part = size // 2

    def block(q, half):
        return out_ref.at[pl.ds(pl.multiple_of(q * size + half * part, part), part)]

    def copy(q, half, target, index, own=False):
        return pltpu.make_async_remote_copy(
            src_ref=x_ref.at[pl.ds(half * part, part)] if own else block(q, half),
            dst_ref=block(q, half),
            send_sem=send_sem.at[index],
            recv_sem=recv_sem.at[q * 2 + half],
            device_id={"clus": target},
        )

    def arrived(q, half):
        copy(q, half, index_of(place, side, 1 - core), 0).wait_recv()

    mine = pltpu.make_async_copy(x_ref, out_ref.at[pl.ds(pl.multiple_of(me * size, size), size)], local_sem)
    mine.start()
    greet(line, place, side, core)

    sends = []

    def send(condition, q, half, target, own=False):
        sends.append((condition, q, half, target, own))
        index = len(sends) - 1

        @pl.when(condition)
        def _():
            copy(q, half, target, index, own).start()

    always = place >= 0
    sibling = index_of(place, side, 1 - core)
    across = index_of(place, 1 - side, core)
    down = index_of(place - 1, side, core)
    up = index_of(place + 1, side, core)

    def pass_on(q, half, here, forward, target):
        @pl.when(here)
        def _():
            arrived(q, half)

        send(here & forward, q, half, target)
        send(here, q, half, across)
        send(here, q, half, sibling)

    def relay(q, half, here):
        @pl.when(here)
        def _():
            arrived(q, half)

        send(here, q, half, sibling)

    for half in range(2):
        send(place < line - 1, me, half, up, True)
        send(place > 0, me, half, down, True)
        send(always, me, half, across, True)
    for half in range(2):
        send(always, me, half, sibling, True)
    width = sketch_ref.shape[1]

    def prepare(i, carry):
        features_ref[i] = row_features(x_ref[i][width:])
        left_ref[i] = left_operand(sketch_ref[i])
        return carry

    lax.fori_loop(0, size, prepare, 0)
    for step in range(1, line + 1):
        for half in range(2):
            if step < line:
                pass_on(
                    index_of(place - step, side, core), half, place >= step, place < line - 1, up
                )
                pass_on(
                    index_of(place + step, side, core), half, place + step < line, place > 0, down
                )
            if step == 1:
                relay(across, half, always)
            else:
                relay(index_of(place - step + 1, 1 - side, core), half, place >= step - 1)
                relay(index_of(place + step - 1, 1 - side, core), half, place + step - 1 < line)
    for z in range(line):
        for s in range(2):
            for half in range(2):
                arrived(index_of(z, s, 1 - core), half)
    for index, (condition, q, half, target, own) in enumerate(sends):

        @pl.when(condition)
        def _(index=index, q=q, half=half, target=target, own=own):
            copy(q, half, target, index, own).wait_send()

    mine.wait()


def gather_clusters(packed, left_sketch, owners):
    line = owners // 4
    cl_dev, width, panels = left_sketch.shape
    shape = (owners * packed.shape[0],) + packed.shape[1:]
    most = 2 * (4 + 3 * 2 * (line - 1) + 1 + 2 * (line - 1))
    return pl.pallas_call(
        functools.partial(gather_kernel, line),
        out_shape=(
            jax.ShapeDtypeStruct(shape, packed.dtype),
            jax.ShapeDtypeStruct((cl_dev, 2 * panels, 96), jnp.bfloat16),
            jax.ShapeDtypeStruct((cl_dev, 2 * width, 2 * panels), jnp.bfloat16),
        ),
        in_specs=[pl.BlockSpec(memory_space=pltpu.VMEM)] * 2,
        out_specs=[pl.BlockSpec(memory_space=pl.ANY)] + [pl.BlockSpec(memory_space=pltpu.VMEM)] * 2,
        scratch_shapes=[
            pltpu.SemaphoreType.DMA((most,)),
            pltpu.SemaphoreType.DMA((2 * owners,)),
            pltpu.SemaphoreType.DMA,
        ],
        compiler_params=pltpu.CompilerParams(
            collective_id=0, has_side_effects=True, vmem_limit_bytes=vmem_budget
        ),
        name="gather_clusters",
    )(packed, left_sketch)


def scatter_kernel(
    line,
    x_ref,
    out_ref,
    own_buf,
    core_buf,
    side_buf,
    low_buf,
    high_buf,
    send_sem,
    own_sem,
    core_sem,
    side_sem,
    low_sem,
    high_sem,
):
    me, core, side, place = neighbours(line)
    size = out_ref.shape[0]

    def block(q):
        return x_ref.at[pl.ds(pl.multiple_of(q * size, size), size)]

    half = place // 2
    order = [3 - 3 * half, 2 - half, 1 - place + 4 * half, place]

    def to_sibling(z, s, index):
        return pltpu.make_async_remote_copy(
            src_ref=block(index_of(z, s, 1 - core)),
            dst_ref=core_buf.at[z * 2 + s],
            send_sem=send_sem.at[index],
            recv_sem=core_sem.at[z * 2 + s],
            device_id={"clus": index_of(place, side, 1 - core)},
        )

    def to_side(z, index):
        return pltpu.make_async_remote_copy(
            src_ref=core_buf.at[z * 2 + 1 - side],
            dst_ref=side_buf.at[z],
            send_sem=send_sem.at[index],
            recv_sem=side_sem.at[z],
            device_id={"clus": index_of(place, 1 - side, core)},
        )

    def along(z, index, buf, sem, target):
        return pltpu.make_async_remote_copy(
            src_ref=side_buf.at[z],
            dst_ref=buf.at[z],
            send_sem=send_sem.at[index],
            recv_sem=sem.at[z],
            device_id={"clus": index_of(target, side, core)},
        )

    def upward(z, index):
        return along(z, index, low_buf, low_sem, place + 1)

    def downward(z, index):
        return along(z, index, high_buf, high_sem, place - 1)

    def fetch(z, s):
        return pltpu.make_async_copy(
            block(index_of(z, s, core)), own_buf.at[z * 2 + s], own_sem.at[z * 2 + s]
        )

    greet(line, place, side, core)
    for k, z in enumerate(order):
        to_sibling(z, 1 - side, 2 * k).start()
        fetch(z, 1 - side).start()
    for k, z in enumerate(order):
        to_sibling(z, side, 2 * k + 1).start()
        fetch(z, side).start()
    for k, z in enumerate(order):
        s = 1 - side
        fetch(z, s).wait()
        to_sibling(z, s, 2 * k).wait_recv()
        core_buf[z * 2 + s] = core_buf[z * 2 + s] + own_buf[z * 2 + s]
        to_side(z, 8 + k).start()
    for k, z in enumerate(order):
        fetch(z, side).wait()
        to_sibling(z, side, 2 * k + 1).wait_recv()
        core_buf[z * 2 + side] = core_buf[z * 2 + side] + own_buf[z * 2 + side]
    for k, z in enumerate(order):
        to_side(z, 8 + k).wait_recv()
        side_buf[z] = side_buf[z] + core_buf[z * 2 + side]
        if k < line - 1:

            @pl.when((z > place) & (place > 0))
            def _(z=z):
                upward(z, 0).wait_recv()
                side_buf[z] = side_buf[z] + low_buf[z]

            @pl.when((z < place) & (place < line - 1))
            def _(z=z):
                downward(z, 0).wait_recv()
                side_buf[z] = side_buf[z] + high_buf[z]

            @pl.when(z > place)
            def _(z=z, k=k):
                upward(z, 12 + k).start()

            @pl.when(z < place)
            def _(z=z, k=k):
                downward(z, 12 + k).start()

    out_ref[...] = side_buf[place]

    @pl.when(place > 0)
    def _():
        upward(place, 0).wait_recv()
        out_ref[...] = out_ref[...] + low_buf[place]

    @pl.when(place < line - 1)
    def _():
        downward(place, 0).wait_recv()
        out_ref[...] = out_ref[...] + high_buf[place]

    for k, z in enumerate(order):
        for j, s in enumerate((1 - side, side)):
            to_sibling(z, s, 2 * k + j).wait_send()
        to_side(z, 8 + k).wait_send()
        if k < line - 1:

            @pl.when(z > place)
            def _(z=z, k=k):
                upward(z, 12 + k).wait_send()

            @pl.when(z < place)
            def _(z=z, k=k):
                downward(z, 12 + k).wait_send()


def scatter_sums(outgoing, owners):
    line = owners // 4
    clusters, width, panels = outgoing.shape
    block = (clusters // owners, width, panels)
    return pl.pallas_call(
        functools.partial(scatter_kernel, line),
        out_shape=jax.ShapeDtypeStruct(block, outgoing.dtype),
        in_specs=[pl.BlockSpec(memory_space=pl.ANY)],
        out_specs=pl.BlockSpec(memory_space=pltpu.VMEM),
        scratch_shapes=[
            pltpu.VMEM((2 * line,) + block, jnp.float32),
            pltpu.VMEM((2 * line,) + block, jnp.float32),
            pltpu.VMEM((line,) + block, jnp.float32),
            pltpu.VMEM((line,) + block, jnp.float32),
            pltpu.VMEM((line,) + block, jnp.float32),
            pltpu.SemaphoreType.DMA((4 * line,)),
            pltpu.SemaphoreType.DMA((2 * line,)),
            pltpu.SemaphoreType.DMA((2 * line,)),
            pltpu.SemaphoreType.DMA((line,)),
            pltpu.SemaphoreType.DMA((line,)),
            pltpu.SemaphoreType.DMA((line,)),
        ],
        compiler_params=pltpu.CompilerParams(
            collective_id=1, has_side_effects=True, vmem_limit_bytes=vmem_budget
        ),
        name="scatter_sums",
    )(outgoing)


def gather_shards(
    point_offsets,
    panel_normals,
    right_sketch,
    left_sketch,
    pair_count,
    pair_rows,
    pair_offset,
    pair_cols,
):
    owners = lax.axis_size("clus")
    position = lax.axis_index("clus")
    cl_dev, width, panels = right_sketch.shape
    spare = jnp.zeros((cl_dev, geometry_rows - 6, panels), jnp.float32)
    packed = jnp.concatenate([right_sketch, point_offsets, panel_normals, spare], axis=1)
    columns, features, left = gather_clusters(packed, left_sketch, owners)
    target = (position + 1 + pair_offset[:, 0]) % owners
    row_sum, outgoing = sketch_pairs(
        pair_count,
        pair_rows,
        position * cl_dev + pair_rows,
        target * cl_dev + pair_cols,
        features,
        left,
        columns,
        width,
    )
    col_sum = scatter_sums(outgoing, owners)
    return (row_sum, col_sum)


def shards(
    point_offsets,
    panel_normals,
    right_sketch,
    left_sketch,
    pair_count,
    pair_rows,
    pair_offset,
    pair_cols,
):
    cl_dev, width, panels = right_sketch.shape
    held = lax.axis_size("clus") * cl_dev * (2 * width + geometry_rows) * panels * 4
    fits = lax.axis_size("clus") == 16 and held + 2**23 <= vmem_budget
    plan = gather_shards if fits else exchange_shards
    return plan(
        point_offsets,
        panel_normals,
        right_sketch,
        left_sketch,
        pair_count,
        pair_rows,
        pair_offset,
        pair_cols,
    )


def solution(mesh):
    return jax.shard_map(
        shards,
        mesh=mesh,
        in_specs=(
            P(("groups", "clus"), None, None),
            P(("groups", "clus"), None, None),
            P(("groups", "clus"), None, None),
            P(("groups", "clus"), None, None),
            P(("groups", "clus")),
            P(("groups", "clus")),
            P(("groups", "clus"), None),
            P(("groups", "clus")),
        ),
        out_specs=(P(("groups", "clus"), None, None), P(("groups", "clus"), None, None)),
        check_vma=False,
    )
```

```python
import functools
import math

import jax
import jax.numpy as jnp
import numpy as np
from jax import lax
from jax.experimental import pallas as pl
from jax.experimental.pallas import tpu as pltpu
from jax.sharding import PartitionSpec as P

wave_number = 8.0
precise = lax.Precision.HIGHEST


def centers_of(cluster_ids):
    return jnp.stack([cluster_ids % 16, cluster_ids // 16 % 8, cluster_ids // 128], axis=1).astype(
        jnp.float32
    )


def kernel_block(row_pts, row_nrm, col_pts, col_nrm):
    separation = row_pts[:, :, :, None] - col_pts[:, :, None, :]
    distance = jnp.sqrt(jnp.sum(separation * separation, axis=1))
    inverse = 1.0 / distance
    along_row = jnp.sum(separation * row_nrm[:, :, :, None], axis=1)
    along_col = jnp.sum(separation * col_nrm[:, :, None, :], axis=1)
    normal_dot = jnp.sum(row_nrm[:, :, :, None] * col_nrm[:, :, None, :], axis=1)
    green_value = inverse / (4.0 * math.pi)
    cosine = jnp.cos(wave_number * distance)
    sine_part = jnp.sin(wave_number * distance)
    slope_real = green_value * (-cosine * inverse - wave_number * sine_part)
    slope_imag = green_value * (-sine_part * inverse + wave_number * cosine)
    double_real = -along_col * inverse * slope_real
    double_imag = -along_col * inverse * slope_imag
    curve_real = 3.0 * inverse * inverse - wave_number * wave_number
    curve_imag = -3.0 * wave_number * inverse
    second_real = green_value * (cosine * curve_real - sine_part * curve_imag)
    second_imag = green_value * (sine_part * curve_real + cosine * curve_imag)
    tangle = along_row * along_col * inverse * inverse
    hyper_real = -(tangle * second_real + normal_dot * inverse * slope_real)
    hyper_imag = -(tangle * second_imag + normal_dot * inverse * slope_imag)
    return (double_real - hyper_imag / wave_number, double_imag + hyper_real / wave_number)


def sketch_pair(kern_real, kern_imag, right_block, left_block):
    halves = right_block.shape[1] // 2
    real_right = jnp.einsum("bak,bik->bai", right_block, kern_real, precision=precise)
    imag_right = jnp.einsum("bak,bik->bai", right_block, kern_imag, precision=precise)
    row_part = jnp.concatenate(
        [
            real_right[:, :halves] - imag_right[:, halves:],
            imag_right[:, :halves] + real_right[:, halves:],
        ],
        axis=1,
    )
    real_left = jnp.einsum("bai,bik->bak", left_block, kern_real, precision=precise)
    imag_left = jnp.einsum("bai,bik->bak", left_block, kern_imag, precision=precise)
    col_part = jnp.concatenate(
        [
            real_left[:, :halves] + imag_left[:, halves:],
            real_left[:, halves:] - imag_left[:, :halves],
        ],
        axis=1,
    )
    return (row_part, col_part)


def exchange_shards(
    point_offsets,
    panel_normals,
    right_sketch,
    left_sketch,
    pair_count,
    pair_rows,
    pair_offset,
    pair_cols,
):
    owners = lax.axis_size("clus")
    position = lax.axis_index("clus")
    cl_dev, width, panels = right_sketch.shape
    slots = pair_rows.shape[0]
    per_peer = max(2, 2 * slots // owners)
    slot_total = owners * per_peer
    local_ids = position * cl_dev + jnp.arange(cl_dev, dtype=jnp.int32)
    cluster_range = jnp.arange(cl_dev, dtype=jnp.int32)
    points = point_offsets + centers_of(local_ids)[:, :, None]
    live_count = pair_count[0]
    slot_index = jnp.arange(slots, dtype=jnp.int32)
    is_live = slot_index < live_count
    target = (position + 1 + pair_offset[:, 0]) % owners
    peer_hits = (target[:, None] == jnp.arange(owners, dtype=jnp.int32)[None, :]).astype(jnp.int32)
    peer_rank = jnp.sum(jnp.cumsum(peer_hits, axis=0) * peer_hits, axis=1) - 1
    send_pos = target * per_peer + peer_rank
    col_global = target * cl_dev + pair_cols
    zero_buffer = jnp.zeros((slot_total, width, panels), jnp.float32)
    zero_local = jnp.zeros((cl_dev, width, panels), jnp.float32)
    col_tags = (
        jnp.full((slot_total,), -1, jnp.int32).at[send_pos].set(jnp.where(is_live, pair_cols, -1))
    )
    incoming = lax.all_to_all(
        col_tags.reshape(owners, per_peer), "clus", split_axis=0, concat_axis=0, tiled=True
    ).reshape(slot_total)
    picked = jnp.maximum(incoming, 0)
    got_pts, got_nrm, got_right = (
        lax.all_to_all(
            point_offsets[picked].reshape(owners, per_peer, 3, panels),
            "clus",
            split_axis=0,
            concat_axis=0,
            tiled=True,
        ),
        lax.all_to_all(
            panel_normals[picked].reshape(owners, per_peer, 3, panels),
            "clus",
            split_axis=0,
            concat_axis=0,
            tiled=True,
        ),
        lax.all_to_all(
            right_sketch[picked].reshape(owners, per_peer, width, panels),
            "clus",
            split_axis=0,
            concat_axis=0,
            tiled=True,
        ),
    )
    got_pts = got_pts.reshape(slot_total, 3, panels)
    got_nrm = got_nrm.reshape(slot_total, 3, panels)
    got_right = got_right.reshape(slot_total, width, panels)

    def owner_step(block_turn, running):
        row_sum, outgoing = running
        block_index = block_turn * 8 + jnp.arange(8, dtype=jnp.int32)
        weight = (block_index < live_count).astype(jnp.float32)
        slot_at = lax.dynamic_slice_in_dim(send_pos, block_turn * 8, 8)
        row_local = lax.dynamic_slice_in_dim(pair_rows, block_turn * 8, 8)
        col_block = lax.dynamic_slice_in_dim(col_global, block_turn * 8, 8)
        col_pts = got_pts[slot_at] + centers_of(col_block)[:, :, None]
        kern_real, kern_imag = kernel_block(
            points[row_local], panel_normals[row_local], col_pts, got_nrm[slot_at]
        )
        row_part, col_part = sketch_pair(
            kern_real, kern_imag, got_right[slot_at], left_sketch[row_local]
        )
        select = (row_local[:, None] == cluster_range[None, :]).astype(jnp.float32) * weight[
            :, None
        ]
        row_sum = row_sum + jnp.einsum("bl,bak->lak", select, row_part, precision=precise)
        outgoing = outgoing.at[slot_at].add(col_part * weight[:, None, None])
        return (row_sum, outgoing)

    turn_count = (live_count + 7) // 8
    row_sum, outgoing = lax.fori_loop(0, turn_count, owner_step, (zero_local, zero_buffer))
    returned = lax.all_to_all(
        outgoing.reshape(owners, per_peer, width, panels),
        "clus",
        split_axis=0,
        concat_axis=0,
        tiled=True,
    ).reshape(slot_total, width, panels)
    select = (incoming[:, None] == cluster_range[None, :]).astype(jnp.float32)
    col_sum = jnp.einsum("sl,sak->lak", select, returned, precision=precise)
    return (row_sum, col_sum)


geometry_rows = 8
unroll = 8
vmem_budget = 40 * 2**20
kernel_scale = wave_number * wave_number / (12.0 * math.pi)


def phase_coefficients():
    def fit(function, degree):
        series = np.polynomial.chebyshev.Chebyshev.interpolate(function, degree, domain=[0.0, 0.25])
        return [float(c) for c in series.convert(kind=np.polynomial.Polynomial).coef]

    def sine_ratio(z):
        return math.sqrt(2.0) * math.pi * np.sinc(np.sqrt(z))

    def cosine(z):
        return math.sqrt(2.0) * np.cos(math.pi * np.sqrt(z))

    return fit(sine_ratio, 3), fit(cosine, 4)


sine_terms, cosine_terms = phase_coefficients()


def horner(terms, z):
    value = terms[-1] * z + terms[-2]
    for term in terms[-3::-1]:
        value = value * z + term
    return value


def split_two(x):
    high = x.astype(jnp.bfloat16)
    return high, (x - high.astype(jnp.float32)).astype(jnp.bfloat16)


def rounded(x):
    return x.astype(jnp.bfloat16).astype(jnp.float32)


def row_features(geometry):
    index = lax.broadcasted_iota(jnp.int32, geometry.shape, 0)
    x = [wave_number * geometry[i : i + 1] for i in range(3)]
    n = [geometry[i : i + 1] for i in range(3, 6)]
    zero = jnp.zeros_like(x[0])
    one = zero + 1.0

    def rows(parts):
        block = jnp.zeros_like(geometry)
        for i, part in parts.items():
            block = jnp.where(index == i, part, block)
        return block

    def form(parts, constant):
        block = rows(parts)
        high = rounded(block)
        low = block - high
        c_high = rounded(constant)
        c_middle = rounded(constant - c_high)
        tail = rows({0: c_high, 1: c_middle, 2: constant - c_high - c_middle})
        return jnp.concatenate([high, high, high, low, low, tail], axis=0)

    square = form(
        {0: -2.0 * x[0], 1: -2.0 * x[1], 2: -2.0 * x[2], 6: one},
        x[0] * x[0] + x[1] * x[1] + x[2] * x[2],
    )
    along_col = form({3: x[0], 4: x[1], 5: x[2], 7: -one}, zero)
    along_row = form({0: -n[0], 1: -n[1], 2: -n[2]}, x[0] * n[0] + x[1] * n[1] + x[2] * n[2])
    normal_dot = form({3: n[0], 4: n[1], 5: n[2]}, zero)
    empty = jnp.zeros((32, geometry.shape[1]), jnp.float32)
    left = jnp.concatenate([square, along_col, empty], axis=0)
    right = jnp.concatenate([along_row, normal_dot, empty], axis=0)
    both = jnp.concatenate([left.T, right.T], axis=0)
    return both[:, :96].astype(jnp.bfloat16)


def left_operand(left):
    halves = left.shape[0] // 2

    def complex_rows(block):
        real, imag = block[:halves], block[halves:]
        return [jnp.concatenate([real, imag], axis=1), jnp.concatenate([imag, -real], axis=1)]

    high, low = split_two(left)
    return jnp.concatenate(complex_rows(high) + complex_rows(low), axis=0)


def pair_parts(features, left, column, width, shift):
    panels = column.shape[1]
    halves = width // 2
    geometry = column[width:]
    index = lax.broadcasted_iota(jnp.int32, geometry.shape, 0)
    move = jnp.where(
        index == 0, shift[0], jnp.where(index == 1, shift[1], jnp.where(index == 2, shift[2], 0.0))
    )
    base = jnp.where(index < 3, wave_number, 1.0) * (geometry + move)
    y = [base[i : i + 1] for i in range(3)]
    m = [base[i : i + 1] for i in range(3, 6)]
    square = y[0] * y[0] + y[1] * y[1] + y[2] * y[2]
    inner = y[0] * m[0] + y[1] * m[1] + y[2] * m[2]
    full = jnp.where(index == 6, square, jnp.where(index == 7, inner, base))
    high = full.astype(jnp.bfloat16).astype(jnp.float32)
    rest = full - high
    middle = rest.astype(jnp.bfloat16).astype(jnp.float32)
    low = rest - middle
    stack = jnp.concatenate([high, middle, low, high, middle, jnp.ones_like(high)], axis=0).astype(
        jnp.bfloat16
    )
    empty = jnp.zeros_like(stack)
    operand = jnp.concatenate(
        [jnp.concatenate([stack, empty], axis=1), jnp.concatenate([empty, stack], axis=1)], axis=0
    )
    forms = jnp.dot(features, operand, preferred_element_type=jnp.float32)

    pieces = []
    chunk = 32
    magic = 1.5 * 2.0**23
    for start in range(0, panels, chunk):
        r2 = forms[start : start + chunk, :panels]
        along_col = forms[start : start + chunk, panels:]
        along_row = forms[panels + start : panels + start + chunk, :panels]
        normal_dot = forms[panels + start : panels + start + chunk, panels:]
        inverse = lax.rsqrt(r2)
        turns = (r2 * inverse) * (0.5 / math.pi)
        turns = turns - ((turns + magic) - magic)
        z = turns * turns
        sine_half = turns * horner(sine_terms, z)
        cosine_half = horner(cosine_terms, z)
        weight = 3.0 * (inverse * inverse)
        scaled = sine_half * weight
        sine_w = scaled * cosine_half
        cosine_w = weight - scaled * sine_half
        both = along_col * along_row
        inner_term = normal_dot - both * weight
        real = inner_term + along_col * inverse
        imag = inverse * (inner_term + both) - along_col
        pieces.append((cosine_w * real - sine_w * imag, cosine_w * imag + sine_w * real))
    real, imag = [jnp.concatenate([piece[q] for piece in pieces], axis=0) for q in range(2)]

    def operand_of(real, imag):
        return jnp.concatenate(
            [jnp.concatenate(split_two(real), axis=1), jnp.concatenate(split_two(imag), axis=1)],
            axis=0,
        )

    w_high, w_low = split_two(column[:width])

    def complex_rows(block):
        real, imag = block[:halves], block[halves:]
        return [jnp.concatenate([real, -imag], axis=1), jnp.concatenate([imag, real], axis=1)]

    right = jnp.concatenate(complex_rows(w_high) + complex_rows(w_low), axis=0)
    row_out = jnp.dot(right, operand_of(real.T, imag.T), preferred_element_type=jnp.float32)
    col_out = jnp.dot(left, operand_of(real, imag), preferred_element_type=jnp.float32)

    def fold(out):
        return (
            out[:width, :panels]
            + out[:width, panels:]
            + (out[width:, :panels] + out[width:, panels:])
        )

    return fold(row_out), fold(col_out)


def pair_kernel(
    live_ref, row_ref, global_row_ref, col_ref, features_ref, left_ref, column_ref, row_out, col_out
):
    row_out[...] = jnp.zeros_like(row_out)
    width = row_out.shape[1]

    def clear(i, carry):
        col_out[i] = jnp.zeros(col_out.shape[1:], jnp.float32)
        return carry

    lax.fori_loop(0, col_out.shape[0], clear, 0)
    live = live_ref[0]

    def center(c):
        return (c & 15, (c >> 4) & 7, c >> 7)

    def turn(step, carry):
        done = []
        for k in range(unroll):
            slot = step * unroll + k
            row = row_ref[slot]
            col = col_ref[slot]
            shift = [
                (b - a).astype(jnp.float32)
                for a, b in zip(center(global_row_ref[slot]), center(col))
            ]
            parts = pair_parts(features_ref[row], left_ref[row], column_ref[col], width, shift)
            scale = jnp.where(slot < live, kernel_scale, 0.0)
            done.append((row, col, parts[0] * scale, parts[1] * scale))
        for row, col, row_part, col_part in done:
            row_out[row] += row_part
            col_out[col] += col_part
        return carry

    lax.fori_loop(0, (live + unroll - 1) // unroll, turn, 0)


def sketch_pairs(live, rows, global_rows, cols, features, left, columns, width):
    cl_dev = features.shape[0]
    clusters, _, panels = columns.shape
    return pl.pallas_call(
        pair_kernel,
        grid_spec=pltpu.PrefetchScalarGridSpec(
            num_scalar_prefetch=4,
            in_specs=[pl.BlockSpec(memory_space=pltpu.VMEM)] * 3,
            out_specs=[pl.BlockSpec(memory_space=pltpu.VMEM)] * 2,
        ),
        out_shape=(
            jax.ShapeDtypeStruct((cl_dev, width, panels), jnp.float32),
            jax.ShapeDtypeStruct((clusters, width, panels), jnp.float32),
        ),
        compiler_params=pltpu.CompilerParams(vmem_limit_bytes=vmem_budget),
        name="pair_sketches",
    )(live, rows, global_rows, cols, features, left, columns)


def neighbours(line):
    me = lax.axis_index("clus")
    core, side, place = me % 2, me // 2 % 2, me // 4
    return me, core, side, place


def index_of(place, side, core):
    return place * 4 + side * 2 + core


def greet(line, place, side, core):
    barrier = pltpu.get_barrier_semaphore()

    def call(target):
        pl.semaphore_signal(barrier, inc=1, device_id={"clus": target})

    call(index_of(place, side, 1 - core))
    call(index_of(place, 1 - side, core))

    @pl.when(place > 0)
    def _():
        call(index_of(place - 1, side, core))

    @pl.when(place < line - 1)
    def _():
        call(index_of(place + 1, side, core))

    pl.semaphore_wait(barrier, 2 + jnp.minimum(place, 1) + jnp.minimum(line - 1 - place, 1))


def gather_kernel(
    line,
    x_ref,
    sketch_ref,
    out_ref,
    features_ref,
    left_ref,
    send_sem,
    recv_sem,
    local_sem,
):
    me, core, side, place = neighbours(line)
    size = x_ref.shape[0]
    part = size // 2

    def block(q, half):
        return out_ref.at[pl.ds(pl.multiple_of(q * size + half * part, part), part)]

    def copy(q, half, target, index, own=False):
        return pltpu.make_async_remote_copy(
            src_ref=x_ref.at[pl.ds(half * part, part)] if own else block(q, half),
            dst_ref=block(q, half),
            send_sem=send_sem.at[index],
            recv_sem=recv_sem.at[q * 2 + half],
            device_id={"clus": target},
        )

    def arrived(q, half):
        copy(q, half, index_of(place, side, 1 - core), 0).wait_recv()

    mine = pltpu.make_async_copy(x_ref, out_ref.at[pl.ds(pl.multiple_of(me * size, size), size)], local_sem)
    mine.start()
    greet(line, place, side, core)

    sends = []

    def send(condition, q, half, target, own=False):
        sends.append((condition, q, half, target, own))
        index = len(sends) - 1

        @pl.when(condition)
        def _():
            copy(q, half, target, index, own).start()

    always = place >= 0
    sibling = index_of(place, side, 1 - core)
    across = index_of(place, 1 - side, core)
    down = index_of(place - 1, side, core)
    up = index_of(place + 1, side, core)

    def pass_on(z, half, here, forward, target):
        q = index_of(z, side, core)

        @pl.when(here)
        def _():
            arrived(q, half)

        send(here & forward, q, half, target)
        send(here & (z > 0) & (z < line - 1) if half else here, q, half, across)
        send(here, q, half, sibling)

    def relay(z, half, here):
        q = index_of(z, 1 - side, core)

        @pl.when(here)
        def _():
            arrived(q, half)

        if half:
            send(here & (z == 0) & (place < line - 1), q, half, up)
            send(here & (z == line - 1) & (place > 0), q, half, down)
        send(here, q, half, sibling)

    for half in range(2):
        send(place < line - 1, me, half, up, True)
        send(place > 0, me, half, down, True)
        send(always, me, half, across, True)
    for half in range(2):
        send(always, me, half, sibling, True)
    width = sketch_ref.shape[1]

    def prepare(i, carry):
        features_ref[i] = row_features(x_ref[i][width:])
        left_ref[i] = left_operand(sketch_ref[i])
        return carry

    lax.fori_loop(0, size, prepare, 0)
    for step in range(1, line + 1):
        for half in range(2):
            if step < line:
                pass_on(place - step, half, place >= step, place < line - 1, up)
                pass_on(place + step, half, place + step < line, place > 0, down)
            if step == 1:
                relay(place, half, always)
            else:
                relay(place - step + 1, half, place >= step - 1)
                relay(place + step - 1, half, place + step - 1 < line)
    for z in range(line):
        for s in range(2):
            for half in range(2):
                arrived(index_of(z, s, 1 - core), half)
    for index, (condition, q, half, target, own) in enumerate(sends):

        @pl.when(condition)
        def _(index=index, q=q, half=half, target=target, own=own):
            copy(q, half, target, index, own).wait_send()

    mine.wait()


def gather_clusters(packed, left_sketch, owners):
    line = owners // 4
    cl_dev, width, panels = left_sketch.shape
    shape = (owners * packed.shape[0],) + packed.shape[1:]
    most = 2 * (4 + 3 * 2 * (line - 1)) + 4 * (1 + 2 * (line - 1))
    return pl.pallas_call(
        functools.partial(gather_kernel, line),
        out_shape=(
            jax.ShapeDtypeStruct(shape, packed.dtype),
            jax.ShapeDtypeStruct((cl_dev, 2 * panels, 96), jnp.bfloat16),
            jax.ShapeDtypeStruct((cl_dev, 2 * width, 2 * panels), jnp.bfloat16),
        ),
        in_specs=[pl.BlockSpec(memory_space=pltpu.VMEM)] * 2,
        out_specs=[pl.BlockSpec(memory_space=pl.ANY)] + [pl.BlockSpec(memory_space=pltpu.VMEM)] * 2,
        scratch_shapes=[
            pltpu.SemaphoreType.DMA((most,)),
            pltpu.SemaphoreType.DMA((2 * owners,)),
            pltpu.SemaphoreType.DMA,
        ],
        compiler_params=pltpu.CompilerParams(
            collective_id=0, has_side_effects=True, vmem_limit_bytes=vmem_budget
        ),
        name="gather_clusters",
    )(packed, left_sketch)


def scatter_kernel(
    line,
    x_ref,
    out_ref,
    own_buf,
    core_buf,
    side_buf,
    low_buf,
    high_buf,
    edge_buf,
    send_sem,
    own_sem,
    core_sem,
    side_sem,
    low_sem,
    high_sem,
    edge_sem,
):
    me, core, side, place = neighbours(line)
    size = out_ref.shape[0]

    def block(q):
        return x_ref.at[pl.ds(pl.multiple_of(q * size, size), size)]

    half = place // 2
    order = [3 - 3 * half, 2 - half, 1 - place + 4 * half, place]

    def to_sibling(z, s, index):
        return pltpu.make_async_remote_copy(
            src_ref=block(index_of(z, s, 1 - core)),
            dst_ref=core_buf.at[z * 2 + s],
            send_sem=send_sem.at[index],
            recv_sem=core_sem.at[z * 2 + s],
            device_id={"clus": index_of(place, side, 1 - core)},
        )

    part = size // 2

    def to_side(z, half, index):
        rows = pl.ds(half * part, part)
        return pltpu.make_async_remote_copy(
            src_ref=core_buf.at[z * 2 + 1 - side, rows],
            dst_ref=side_buf.at[z, rows],
            send_sem=send_sem.at[index],
            recv_sem=side_sem.at[z * 2 + half],
            device_id={"clus": index_of(place, 1 - side, core)},
        )

    def crosses(z):
        return (z > 0) & (z < line - 1)

    def to_edge(end, index):
        return pltpu.make_async_remote_copy(
            src_ref=core_buf.at[end * 2 + 1 - side, pl.ds(part, part)],
            dst_ref=edge_buf.at[min(end, 1)],
            send_sem=send_sem.at[index],
            recv_sem=edge_sem.at[min(end, 1)],
            device_id={"clus": index_of(place + (1 if end else -1), side, core)},
        )

    def along(z, index, buf, sem, target):
        return pltpu.make_async_remote_copy(
            src_ref=side_buf.at[z],
            dst_ref=buf.at[z],
            send_sem=send_sem.at[index],
            recv_sem=sem.at[z],
            device_id={"clus": index_of(target, side, core)},
        )

    def upward(z, index):
        return along(z, index, low_buf, low_sem, place + 1)

    def downward(z, index):
        return along(z, index, high_buf, high_sem, place - 1)

    def fetch(z, s):
        return pltpu.make_async_copy(
            block(index_of(z, s, core)), own_buf.at[z * 2 + s], own_sem.at[z * 2 + s]
        )

    greet(line, place, side, core)
    for k, z in enumerate(order):
        to_sibling(z, 1 - side, 2 * k).start()
        fetch(z, 1 - side).start()
    for k, z in enumerate(order):
        to_sibling(z, side, 2 * k + 1).start()
        fetch(z, side).start()
    for k, z in enumerate(order):
        s = 1 - side
        fetch(z, s).wait()
        to_sibling(z, s, 2 * k).wait_recv()
        core_buf[z * 2 + s] = core_buf[z * 2 + s] + own_buf[z * 2 + s]
        to_side(z, 0, 8 + k).start()

        @pl.when(crosses(z))
        def _(z=z, k=k):
            to_side(z, 1, 15 + k).start()

    for e, end in enumerate((0, line - 1)):
        far = line - 1 - end

        @pl.when(place != far)
        def _(end=end, e=e):
            to_edge(end, 0).wait_recv()
            rows = pl.ds(part, part)
            core_buf[end * 2 + 1 - side, rows] = core_buf[end * 2 + 1 - side, rows] + edge_buf[e]

        @pl.when(place != end)
        def _(end=end, e=e):
            to_edge(end, 19 + e).start()

        @pl.when(place == end)
        def _(end=end, e=e):
            to_side(end, 1, 21 + e).start()

    for k, z in enumerate(order):
        fetch(z, side).wait()
        to_sibling(z, side, 2 * k + 1).wait_recv()
        core_buf[z * 2 + side] = core_buf[z * 2 + side] + own_buf[z * 2 + side]
    for k, z in enumerate(order):
        first, second = pl.ds(0, part), pl.ds(part, part)
        to_side(z, 0, 0).wait_recv()
        side_buf[z, first] = side_buf[z, first] + core_buf[z * 2 + side, first]

        @pl.when(crosses(z) | (z == place))
        def _(z=z, second=second):
            to_side(z, 1, 0).wait_recv()
            side_buf[z, second] = side_buf[z, second] + core_buf[z * 2 + side, second]

        @pl.when(jnp.logical_not(crosses(z) | (z == place)))
        def _(z=z, second=second):
            side_buf[z, second] = core_buf[z * 2 + side, second]

        if k < line - 1:

            @pl.when((z > place) & (place > 0))
            def _(z=z):
                upward(z, 0).wait_recv()
                side_buf[z] = side_buf[z] + low_buf[z]

            @pl.when((z < place) & (place < line - 1))
            def _(z=z):
                downward(z, 0).wait_recv()
                side_buf[z] = side_buf[z] + high_buf[z]

            @pl.when(z > place)
            def _(z=z, k=k):
                upward(z, 12 + k).start()

            @pl.when(z < place)
            def _(z=z, k=k):
                downward(z, 12 + k).start()

    out_ref[...] = side_buf[place]

    @pl.when(place > 0)
    def _():
        upward(place, 0).wait_recv()
        out_ref[...] = out_ref[...] + low_buf[place]

    @pl.when(place < line - 1)
    def _():
        downward(place, 0).wait_recv()
        out_ref[...] = out_ref[...] + high_buf[place]

    for k, z in enumerate(order):
        for j, s in enumerate((1 - side, side)):
            to_sibling(z, s, 2 * k + j).wait_send()
        to_side(z, 0, 8 + k).wait_send()

        @pl.when(crosses(z))
        def _(z=z, k=k):
            to_side(z, 1, 15 + k).wait_send()

        if k < line - 1:

            @pl.when(z > place)
            def _(z=z, k=k):
                upward(z, 12 + k).wait_send()

            @pl.when(z < place)
            def _(z=z, k=k):
                downward(z, 12 + k).wait_send()

    for e, end in enumerate((0, line - 1)):

        @pl.when(place != end)
        def _(end=end, e=e):
            to_edge(end, 19 + e).wait_send()

        @pl.when(place == end)
        def _(end=end, e=e):
            to_side(end, 1, 21 + e).wait_send()


def scatter_sums(outgoing, owners):
    line = owners // 4
    clusters, width, panels = outgoing.shape
    block = (clusters // owners, width, panels)
    return pl.pallas_call(
        functools.partial(scatter_kernel, line),
        out_shape=jax.ShapeDtypeStruct(block, outgoing.dtype),
        in_specs=[pl.BlockSpec(memory_space=pl.ANY)],
        out_specs=pl.BlockSpec(memory_space=pltpu.VMEM),
        scratch_shapes=[
            pltpu.VMEM((2 * line,) + block, jnp.float32),
            pltpu.VMEM((2 * line,) + block, jnp.float32),
            pltpu.VMEM((line,) + block, jnp.float32),
            pltpu.VMEM((line,) + block, jnp.float32),
            pltpu.VMEM((line,) + block, jnp.float32),
            pltpu.VMEM((2, block[0] // 2) + block[1:], jnp.float32),
            pltpu.SemaphoreType.DMA((23,)),
            pltpu.SemaphoreType.DMA((2 * line,)),
            pltpu.SemaphoreType.DMA((2 * line,)),
            pltpu.SemaphoreType.DMA((2 * line,)),
            pltpu.SemaphoreType.DMA((line,)),
            pltpu.SemaphoreType.DMA((line,)),
            pltpu.SemaphoreType.DMA((2,)),
        ],
        compiler_params=pltpu.CompilerParams(
            collective_id=1, has_side_effects=True, vmem_limit_bytes=vmem_budget
        ),
        name="scatter_sums",
    )(outgoing)


def gather_shards(
    point_offsets,
    panel_normals,
    right_sketch,
    left_sketch,
    pair_count,
    pair_rows,
    pair_offset,
    pair_cols,
):
    owners = lax.axis_size("clus")
    position = lax.axis_index("clus")
    cl_dev, width, panels = right_sketch.shape
    spare = jnp.zeros((cl_dev, geometry_rows - 6, panels), jnp.float32)
    packed = jnp.concatenate([right_sketch, point_offsets, panel_normals, spare], axis=1)
    columns, features, left = gather_clusters(packed, left_sketch, owners)
    target = (position + 1 + pair_offset[:, 0]) % owners
    row_sum, outgoing = sketch_pairs(
        pair_count,
        pair_rows,
        position * cl_dev + pair_rows,
        target * cl_dev + pair_cols,
        features,
        left,
        columns,
        width,
    )
    col_sum = scatter_sums(outgoing, owners)
    return (row_sum, col_sum)


def shards(
    point_offsets,
    panel_normals,
    right_sketch,
    left_sketch,
    pair_count,
    pair_rows,
    pair_offset,
    pair_cols,
):
    cl_dev, width, panels = right_sketch.shape
    held = lax.axis_size("clus") * cl_dev * (2 * width + geometry_rows) * panels * 4
    fits = lax.axis_size("clus") == 16 and held + 2**23 <= vmem_budget
    plan = gather_shards if fits else exchange_shards
    return plan(
        point_offsets,
        panel_normals,
        right_sketch,
        left_sketch,
        pair_count,
        pair_rows,
        pair_offset,
        pair_cols,
    )


def solution(mesh):
    return jax.shard_map(
        shards,
        mesh=mesh,
        in_specs=(
            P(("groups", "clus"), None, None),
            P(("groups", "clus"), None, None),
            P(("groups", "clus"), None, None),
            P(("groups", "clus"), None, None),
            P(("groups", "clus")),
            P(("groups", "clus")),
            P(("groups", "clus"), None),
            P(("groups", "clus")),
        ),
        out_specs=(P(("groups", "clus"), None, None), P(("groups", "clus"), None, None)),
        check_vma=False,
    )
```

```python
import functools
import math

import jax
import jax.numpy as jnp
import numpy as np
from jax import lax
from jax.experimental import pallas as pl
from jax.experimental.pallas import tpu as pltpu
from jax.sharding import PartitionSpec as P

wave_number = 8.0
precise = lax.Precision.HIGHEST


def centers_of(cluster_ids):
    return jnp.stack([cluster_ids % 16, cluster_ids // 16 % 8, cluster_ids // 128], axis=1).astype(
        jnp.float32
    )


def kernel_block(row_pts, row_nrm, col_pts, col_nrm):
    separation = row_pts[:, :, :, None] - col_pts[:, :, None, :]
    distance = jnp.sqrt(jnp.sum(separation * separation, axis=1))
    inverse = 1.0 / distance
    along_row = jnp.sum(separation * row_nrm[:, :, :, None], axis=1)
    along_col = jnp.sum(separation * col_nrm[:, :, None, :], axis=1)
    normal_dot = jnp.sum(row_nrm[:, :, :, None] * col_nrm[:, :, None, :], axis=1)
    green_value = inverse / (4.0 * math.pi)
    cosine = jnp.cos(wave_number * distance)
    sine_part = jnp.sin(wave_number * distance)
    slope_real = green_value * (-cosine * inverse - wave_number * sine_part)
    slope_imag = green_value * (-sine_part * inverse + wave_number * cosine)
    double_real = -along_col * inverse * slope_real
    double_imag = -along_col * inverse * slope_imag
    curve_real = 3.0 * inverse * inverse - wave_number * wave_number
    curve_imag = -3.0 * wave_number * inverse
    second_real = green_value * (cosine * curve_real - sine_part * curve_imag)
    second_imag = green_value * (sine_part * curve_real + cosine * curve_imag)
    tangle = along_row * along_col * inverse * inverse
    hyper_real = -(tangle * second_real + normal_dot * inverse * slope_real)
    hyper_imag = -(tangle * second_imag + normal_dot * inverse * slope_imag)
    return (double_real - hyper_imag / wave_number, double_imag + hyper_real / wave_number)


def sketch_pair(kern_real, kern_imag, right_block, left_block):
    halves = right_block.shape[1] // 2
    real_right = jnp.einsum("bak,bik->bai", right_block, kern_real, precision=precise)
    imag_right = jnp.einsum("bak,bik->bai", right_block, kern_imag, precision=precise)
    row_part = jnp.concatenate(
        [
            real_right[:, :halves] - imag_right[:, halves:],
            imag_right[:, :halves] + real_right[:, halves:],
        ],
        axis=1,
    )
    real_left = jnp.einsum("bai,bik->bak", left_block, kern_real, precision=precise)
    imag_left = jnp.einsum("bai,bik->bak", left_block, kern_imag, precision=precise)
    col_part = jnp.concatenate(
        [
            real_left[:, :halves] + imag_left[:, halves:],
            real_left[:, halves:] - imag_left[:, :halves],
        ],
        axis=1,
    )
    return (row_part, col_part)


def exchange_shards(
    point_offsets,
    panel_normals,
    right_sketch,
    left_sketch,
    pair_count,
    pair_rows,
    pair_offset,
    pair_cols,
):
    owners = lax.axis_size("clus")
    position = lax.axis_index("clus")
    cl_dev, width, panels = right_sketch.shape
    slots = pair_rows.shape[0]
    per_peer = max(2, 2 * slots // owners)
    slot_total = owners * per_peer
    local_ids = position * cl_dev + jnp.arange(cl_dev, dtype=jnp.int32)
    cluster_range = jnp.arange(cl_dev, dtype=jnp.int32)
    points = point_offsets + centers_of(local_ids)[:, :, None]
    live_count = pair_count[0]
    slot_index = jnp.arange(slots, dtype=jnp.int32)
    is_live = slot_index < live_count
    target = (position + 1 + pair_offset[:, 0]) % owners
    peer_hits = (target[:, None] == jnp.arange(owners, dtype=jnp.int32)[None, :]).astype(jnp.int32)
    peer_rank = jnp.sum(jnp.cumsum(peer_hits, axis=0) * peer_hits, axis=1) - 1
    send_pos = target * per_peer + peer_rank
    col_global = target * cl_dev + pair_cols
    zero_buffer = jnp.zeros((slot_total, width, panels), jnp.float32)
    zero_local = jnp.zeros((cl_dev, width, panels), jnp.float32)
    col_tags = (
        jnp.full((slot_total,), -1, jnp.int32).at[send_pos].set(jnp.where(is_live, pair_cols, -1))
    )
    incoming = lax.all_to_all(
        col_tags.reshape(owners, per_peer), "clus", split_axis=0, concat_axis=0, tiled=True
    ).reshape(slot_total)
    picked = jnp.maximum(incoming, 0)
    got_pts, got_nrm, got_right = (
        lax.all_to_all(
            point_offsets[picked].reshape(owners, per_peer, 3, panels),
            "clus",
            split_axis=0,
            concat_axis=0,
            tiled=True,
        ),
        lax.all_to_all(
            panel_normals[picked].reshape(owners, per_peer, 3, panels),
            "clus",
            split_axis=0,
            concat_axis=0,
            tiled=True,
        ),
        lax.all_to_all(
            right_sketch[picked].reshape(owners, per_peer, width, panels),
            "clus",
            split_axis=0,
            concat_axis=0,
            tiled=True,
        ),
    )
    got_pts = got_pts.reshape(slot_total, 3, panels)
    got_nrm = got_nrm.reshape(slot_total, 3, panels)
    got_right = got_right.reshape(slot_total, width, panels)

    def owner_step(block_turn, running):
        row_sum, outgoing = running
        block_index = block_turn * 8 + jnp.arange(8, dtype=jnp.int32)
        weight = (block_index < live_count).astype(jnp.float32)
        slot_at = lax.dynamic_slice_in_dim(send_pos, block_turn * 8, 8)
        row_local = lax.dynamic_slice_in_dim(pair_rows, block_turn * 8, 8)
        col_block = lax.dynamic_slice_in_dim(col_global, block_turn * 8, 8)
        col_pts = got_pts[slot_at] + centers_of(col_block)[:, :, None]
        kern_real, kern_imag = kernel_block(
            points[row_local], panel_normals[row_local], col_pts, got_nrm[slot_at]
        )
        row_part, col_part = sketch_pair(
            kern_real, kern_imag, got_right[slot_at], left_sketch[row_local]
        )
        select = (row_local[:, None] == cluster_range[None, :]).astype(jnp.float32) * weight[
            :, None
        ]
        row_sum = row_sum + jnp.einsum("bl,bak->lak", select, row_part, precision=precise)
        outgoing = outgoing.at[slot_at].add(col_part * weight[:, None, None])
        return (row_sum, outgoing)

    turn_count = (live_count + 7) // 8
    row_sum, outgoing = lax.fori_loop(0, turn_count, owner_step, (zero_local, zero_buffer))
    returned = lax.all_to_all(
        outgoing.reshape(owners, per_peer, width, panels),
        "clus",
        split_axis=0,
        concat_axis=0,
        tiled=True,
    ).reshape(slot_total, width, panels)
    select = (incoming[:, None] == cluster_range[None, :]).astype(jnp.float32)
    col_sum = jnp.einsum("sl,sak->lak", select, returned, precision=precise)
    return (row_sum, col_sum)


geometry_rows = 8
unroll = 8
vmem_budget = 40 * 2**20
kernel_scale = wave_number * wave_number / (12.0 * math.pi)


def phase_coefficients():
    def fit(function, degree):
        series = np.polynomial.chebyshev.Chebyshev.interpolate(function, degree, domain=[0.0, 0.25])
        return [float(c) for c in series.convert(kind=np.polynomial.Polynomial).coef]

    def sine_ratio(z):
        return math.sqrt(2.0) * math.pi * np.sinc(np.sqrt(z))

    def cosine(z):
        return math.sqrt(2.0) * np.cos(math.pi * np.sqrt(z))

    return fit(sine_ratio, 3), fit(cosine, 4)


sine_terms, cosine_terms = phase_coefficients()


def horner(terms, z):
    value = terms[-1] * z + terms[-2]
    for term in terms[-3::-1]:
        value = value * z + term
    return value


def split_two(x):
    high = x.astype(jnp.bfloat16)
    return high, (x - high.astype(jnp.float32)).astype(jnp.bfloat16)


def rounded(x):
    return x.astype(jnp.bfloat16).astype(jnp.float32)


def row_features(geometry):
    index = lax.broadcasted_iota(jnp.int32, geometry.shape, 0)
    x = [wave_number * geometry[i : i + 1] for i in range(3)]
    n = [geometry[i : i + 1] for i in range(3, 6)]
    zero = jnp.zeros_like(x[0])
    one = zero + 1.0

    def rows(parts):
        block = jnp.zeros_like(geometry)
        for i, part in parts.items():
            block = jnp.where(index == i, part, block)
        return block

    def form(parts, constant):
        block = rows(parts)
        high = rounded(block)
        low = block - high
        c_high = rounded(constant)
        c_middle = rounded(constant - c_high)
        tail = rows({0: c_high, 1: c_middle, 2: constant - c_high - c_middle})
        return jnp.concatenate([high, high, high, low, low, tail], axis=0)

    square = form(
        {0: -2.0 * x[0], 1: -2.0 * x[1], 2: -2.0 * x[2], 6: one},
        x[0] * x[0] + x[1] * x[1] + x[2] * x[2],
    )
    along_col = form({3: x[0], 4: x[1], 5: x[2], 7: -one}, zero)
    along_row = form({0: -n[0], 1: -n[1], 2: -n[2]}, x[0] * n[0] + x[1] * n[1] + x[2] * n[2])
    normal_dot = form({3: n[0], 4: n[1], 5: n[2]}, zero)
    empty = jnp.zeros((32, geometry.shape[1]), jnp.float32)
    left = jnp.concatenate([square, along_col, empty], axis=0)
    right = jnp.concatenate([along_row, normal_dot, empty], axis=0)
    both = jnp.concatenate([left.T, right.T], axis=0)
    return both[:, :96].astype(jnp.bfloat16)


def left_operand(left):
    halves = left.shape[0] // 2

    def complex_rows(block):
        real, imag = block[:halves], block[halves:]
        return [jnp.concatenate([real, imag], axis=1), jnp.concatenate([imag, -real], axis=1)]

    high, low = split_two(left)
    return jnp.concatenate(complex_rows(high) + complex_rows(low), axis=0)


def pair_parts(features, left, column, width, shift):
    panels = column.shape[1]
    halves = width // 2
    geometry = column[width:]
    index = lax.broadcasted_iota(jnp.int32, geometry.shape, 0)
    move = jnp.where(
        index == 0, shift[0], jnp.where(index == 1, shift[1], jnp.where(index == 2, shift[2], 0.0))
    )
    base = jnp.where(index < 3, wave_number, 1.0) * (geometry + move)
    y = [base[i : i + 1] for i in range(3)]
    m = [base[i : i + 1] for i in range(3, 6)]
    square = y[0] * y[0] + y[1] * y[1] + y[2] * y[2]
    inner = y[0] * m[0] + y[1] * m[1] + y[2] * m[2]
    full = jnp.where(index == 6, square, jnp.where(index == 7, inner, base))
    high = full.astype(jnp.bfloat16).astype(jnp.float32)
    rest = full - high
    middle = rest.astype(jnp.bfloat16).astype(jnp.float32)
    low = rest - middle
    stack = jnp.concatenate([high, middle, low, high, middle, jnp.ones_like(high)], axis=0).astype(
        jnp.bfloat16
    )
    empty = jnp.zeros_like(stack)
    operand = jnp.concatenate(
        [jnp.concatenate([stack, empty], axis=1), jnp.concatenate([empty, stack], axis=1)], axis=0
    )
    forms = jnp.dot(features, operand, preferred_element_type=jnp.float32)

    pieces = []
    chunk = 32
    magic = 1.5 * 2.0**23
    for start in range(0, panels, chunk):
        r2 = forms[start : start + chunk, :panels]
        along_col = forms[start : start + chunk, panels:]
        along_row = forms[panels + start : panels + start + chunk, :panels]
        normal_dot = forms[panels + start : panels + start + chunk, panels:]
        inverse = lax.rsqrt(r2)
        turns = (r2 * inverse) * (0.5 / math.pi)
        turns = turns - ((turns + magic) - magic)
        z = turns * turns
        sine_half = turns * horner(sine_terms, z)
        cosine_half = horner(cosine_terms, z)
        weight = 3.0 * (inverse * inverse)
        scaled = sine_half * weight
        sine_w = scaled * cosine_half
        cosine_w = weight - scaled * sine_half
        both = along_col * along_row
        inner_term = normal_dot - both * weight
        real = inner_term + along_col * inverse
        imag = inverse * (inner_term + both) - along_col
        pieces.append((cosine_w * real - sine_w * imag, cosine_w * imag + sine_w * real))
    real, imag = [jnp.concatenate([piece[q] for piece in pieces], axis=0) for q in range(2)]

    def operand_of(real, imag):
        return jnp.concatenate(
            [jnp.concatenate(split_two(real), axis=1), jnp.concatenate(split_two(imag), axis=1)],
            axis=0,
        )

    w_high, w_low = split_two(column[:width])

    def complex_rows(block):
        real, imag = block[:halves], block[halves:]
        return [jnp.concatenate([real, -imag], axis=1), jnp.concatenate([imag, real], axis=1)]

    right = jnp.concatenate(complex_rows(w_high) + complex_rows(w_low), axis=0)
    row_out = jnp.dot(right, operand_of(real.T, imag.T), preferred_element_type=jnp.float32)
    col_out = jnp.dot(left, operand_of(real, imag), preferred_element_type=jnp.float32)

    def fold(out):
        return (
            out[:width, :panels]
            + out[:width, panels:]
            + (out[width:, :panels] + out[width:, panels:])
        )

    return fold(row_out), fold(col_out)


def pair_kernel(
    live_ref, row_ref, global_row_ref, col_ref, features_ref, left_ref, column_ref, row_out, col_out
):
    row_out[...] = jnp.zeros_like(row_out)
    width = row_out.shape[1]

    def clear(i, carry):
        col_out[i] = jnp.zeros(col_out.shape[1:], jnp.float32)
        return carry

    lax.fori_loop(0, col_out.shape[0], clear, 0)
    live = live_ref[0]

    def center(c):
        return (c & 15, (c >> 4) & 7, c >> 7)

    def turn(step, carry):
        done = []
        for k in range(unroll):
            slot = step * unroll + k
            row = row_ref[slot]
            col = col_ref[slot]
            shift = [
                (b - a).astype(jnp.float32)
                for a, b in zip(center(global_row_ref[slot]), center(col))
            ]
            parts = pair_parts(features_ref[row], left_ref[row], column_ref[col], width, shift)
            scale = jnp.where(slot < live, kernel_scale, 0.0)
            done.append((row, col, parts[0] * scale, parts[1] * scale))
        for row, col, row_part, col_part in done:
            row_out[row] += row_part
            col_out[col] += col_part
        return carry

    lax.fori_loop(0, (live + unroll - 1) // unroll, turn, 0)


def sketch_pairs(live, rows, global_rows, cols, features, left, columns, width):
    cl_dev = features.shape[0]
    clusters, _, panels = columns.shape
    return pl.pallas_call(
        pair_kernel,
        grid_spec=pltpu.PrefetchScalarGridSpec(
            num_scalar_prefetch=4,
            in_specs=[pl.BlockSpec(memory_space=pltpu.VMEM)] * 3,
            out_specs=[pl.BlockSpec(memory_space=pltpu.VMEM)] * 2,
        ),
        out_shape=(
            jax.ShapeDtypeStruct((cl_dev, width, panels), jnp.float32),
            jax.ShapeDtypeStruct((clusters, width, panels), jnp.float32),
        ),
        compiler_params=pltpu.CompilerParams(vmem_limit_bytes=vmem_budget),
        name="pair_sketches",
    )(live, rows, global_rows, cols, features, left, columns)


def neighbours(line):
    me = lax.axis_index("clus")
    core, side, place = me % 2, me // 2 % 2, me // 4
    return me, core, side, place


def index_of(place, side, core):
    return place * 4 + side * 2 + core


def greet(line, place, side, core):
    barrier = pltpu.get_barrier_semaphore()

    def call(target):
        pl.semaphore_signal(barrier, inc=1, device_id={"clus": target})

    call(index_of(place, side, 1 - core))
    call(index_of(place, 1 - side, core))

    @pl.when(place > 0)
    def _():
        call(index_of(place - 1, side, core))

    @pl.when(place < line - 1)
    def _():
        call(index_of(place + 1, side, core))

    pl.semaphore_wait(barrier, 2 + jnp.minimum(place, 1) + jnp.minimum(line - 1 - place, 1))


def gather_kernel(
    line,
    x_ref,
    sketch_ref,
    out_ref,
    features_ref,
    left_ref,
    send_sem,
    recv_sem,
    local_sem,
):
    me, core, side, place = neighbours(line)
    size = x_ref.shape[0]
    part = size // 2

    def block(q, half):
        return out_ref.at[pl.ds(pl.multiple_of(q * size + half * part, part), part)]

    def copy(q, half, target, index, own=False):
        return pltpu.make_async_remote_copy(
            src_ref=x_ref.at[pl.ds(half * part, part)] if own else block(q, half),
            dst_ref=block(q, half),
            send_sem=send_sem.at[index],
            recv_sem=recv_sem.at[q * 2 + half],
            device_id={"clus": target},
        )

    def arrived(q, half):
        copy(q, half, index_of(place, side, 1 - core), 0).wait_recv()

    mine = pltpu.make_async_copy(x_ref, out_ref.at[pl.ds(pl.multiple_of(me * size, size), size)], local_sem)
    mine.start()
    greet(line, place, side, core)

    sends = []

    def send(condition, q, half, target, own=False):
        sends.append((condition, q, half, target, own))
        index = len(sends) - 1

        @pl.when(condition)
        def _():
            copy(q, half, target, index, own).start()

    always = place >= 0
    sibling = index_of(place, side, 1 - core)
    across = index_of(place, 1 - side, core)
    down = index_of(place - 1, side, core)
    up = index_of(place + 1, side, core)

    def pass_on(z, half, here, forward, target):
        q = index_of(z, side, core)

        @pl.when(here)
        def _():
            arrived(q, half)

        send(here & forward, q, half, target)
        send(here & (z > 0) & (z < line - 1) if half else here, q, half, across)
        send(here, q, half, sibling)

    def relay(z, half, here):
        q = index_of(z, 1 - side, core)

        @pl.when(here)
        def _():
            arrived(q, half)

        if half:
            send(here & (z == 0) & (place < line - 1), q, half, up)
            send(here & (z == line - 1) & (place > 0), q, half, down)
        send(here, q, half, sibling)

    for half in range(2):
        send(place < line - 1, me, half, up, True)
        send(place > 0, me, half, down, True)
        send(always, me, half, across, True)
    for half in range(2):
        send(always, me, half, sibling, True)
    width = sketch_ref.shape[1]

    def prepare(i, carry):
        features_ref[i] = row_features(x_ref[i][width:])
        left_ref[i] = left_operand(sketch_ref[i])
        return carry

    lax.fori_loop(0, size, prepare, 0)
    for step in range(1, line + 1):
        for half in range(2):
            if step < line:
                pass_on(place - step, half, place >= step, place < line - 1, up)
                pass_on(place + step, half, place + step < line, place > 0, down)
            if step == 1:
                relay(place, half, always)
            else:
                relay(place - step + 1, half, place >= step - 1)
                relay(place + step - 1, half, place + step - 1 < line)
    for z in range(line):
        for s in range(2):
            for half in range(2):
                arrived(index_of(z, s, 1 - core), half)
    for index, (condition, q, half, target, own) in enumerate(sends):

        @pl.when(condition)
        def _(index=index, q=q, half=half, target=target, own=own):
            copy(q, half, target, index, own).wait_send()

    mine.wait()


def gather_clusters(packed, left_sketch, owners):
    line = owners // 4
    cl_dev, width, panels = left_sketch.shape
    shape = (owners * packed.shape[0],) + packed.shape[1:]
    most = 2 * (4 + 3 * 2 * (line - 1)) + 4 * (1 + 2 * (line - 1))
    return pl.pallas_call(
        functools.partial(gather_kernel, line),
        out_shape=(
            jax.ShapeDtypeStruct(shape, packed.dtype),
            jax.ShapeDtypeStruct((cl_dev, 2 * panels, 96), jnp.bfloat16),
            jax.ShapeDtypeStruct((cl_dev, 2 * width, 2 * panels), jnp.bfloat16),
        ),
        in_specs=[pl.BlockSpec(memory_space=pltpu.VMEM)] * 2,
        out_specs=[pl.BlockSpec(memory_space=pl.ANY)] + [pl.BlockSpec(memory_space=pltpu.VMEM)] * 2,
        scratch_shapes=[
            pltpu.SemaphoreType.DMA((most,)),
            pltpu.SemaphoreType.DMA((2 * owners,)),
            pltpu.SemaphoreType.DMA,
        ],
        compiler_params=pltpu.CompilerParams(
            collective_id=0, has_side_effects=True, vmem_limit_bytes=vmem_budget
        ),
        name="gather_clusters",
    )(packed, left_sketch)


def scatter_kernel(
    line,
    x_ref,
    out_ref,
    own_buf,
    core_buf,
    side_buf,
    low_buf,
    high_buf,
    send_sem,
    own_sem,
    core_sem,
    side_sem,
    low_sem,
    high_sem,
):
    me, core, side, place = neighbours(line)
    size = out_ref.shape[0]

    def block(q):
        return x_ref.at[pl.ds(pl.multiple_of(q * size, size), size)]

    half = place // 2
    order = [3 - 3 * half, 2 - half, 1 - place + 4 * half, place]

    def to_sibling(z, s, index):
        return pltpu.make_async_remote_copy(
            src_ref=block(index_of(z, s, 1 - core)),
            dst_ref=core_buf.at[z * 2 + s],
            send_sem=send_sem.at[index],
            recv_sem=core_sem.at[z * 2 + s],
            device_id={"clus": index_of(place, side, 1 - core)},
        )

    def to_side(z, index):
        return pltpu.make_async_remote_copy(
            src_ref=core_buf.at[z * 2 + 1 - side],
            dst_ref=side_buf.at[z],
            send_sem=send_sem.at[index],
            recv_sem=side_sem.at[z],
            device_id={"clus": index_of(place, 1 - side, core)},
        )

    def along(z, index, buf, sem, target):
        return pltpu.make_async_remote_copy(
            src_ref=side_buf.at[z],
            dst_ref=buf.at[z],
            send_sem=send_sem.at[index],
            recv_sem=sem.at[z],
            device_id={"clus": index_of(target, side, core)},
        )

    def upward(z, index):
        return along(z, index, low_buf, low_sem, place + 1)

    def downward(z, index):
        return along(z, index, high_buf, high_sem, place - 1)

    def fetch(z, s):
        return pltpu.make_async_copy(
            block(index_of(z, s, core)), own_buf.at[z * 2 + s], own_sem.at[z * 2 + s]
        )

    greet(line, place, side, core)
    for k, z in enumerate(order):
        to_sibling(z, 1 - side, 2 * k).start()
        fetch(z, 1 - side).start()
    for k, z in enumerate(order):
        to_sibling(z, side, 2 * k + 1).start()
        fetch(z, side).start()
    for k, z in enumerate(order):
        s = 1 - side
        fetch(z, s).wait()
        to_sibling(z, s, 2 * k).wait_recv()
        core_buf[z * 2 + s] = core_buf[z * 2 + s] + own_buf[z * 2 + s]
        to_side(z, 8 + k).start()
    for k, z in enumerate(order):
        fetch(z, side).wait()
        to_sibling(z, side, 2 * k + 1).wait_recv()
        core_buf[z * 2 + side] = core_buf[z * 2 + side] + own_buf[z * 2 + side]
    for k, z in enumerate(order):
        to_side(z, 8 + k).wait_recv()
        side_buf[z] = side_buf[z] + core_buf[z * 2 + side]
        if k < line - 1:

            @pl.when((z > place) & (place > 0))
            def _(z=z):
                upward(z, 0).wait_recv()
                side_buf[z] = side_buf[z] + low_buf[z]

            @pl.when((z < place) & (place < line - 1))
            def _(z=z):
                downward(z, 0).wait_recv()
                side_buf[z] = side_buf[z] + high_buf[z]

            @pl.when(z > place)
            def _(z=z, k=k):
                upward(z, 12 + k).start()

            @pl.when(z < place)
            def _(z=z, k=k):
                downward(z, 12 + k).start()

    out_ref[...] = side_buf[place]

    @pl.when(place > 0)
    def _():
        upward(place, 0).wait_recv()
        out_ref[...] = out_ref[...] + low_buf[place]

    @pl.when(place < line - 1)
    def _():
        downward(place, 0).wait_recv()
        out_ref[...] = out_ref[...] + high_buf[place]

    for k, z in enumerate(order):
        for j, s in enumerate((1 - side, side)):
            to_sibling(z, s, 2 * k + j).wait_send()
        to_side(z, 8 + k).wait_send()
        if k < line - 1:

            @pl.when(z > place)
            def _(z=z, k=k):
                upward(z, 12 + k).wait_send()

            @pl.when(z < place)
            def _(z=z, k=k):
                downward(z, 12 + k).wait_send()


def scatter_sums(outgoing, owners):
    line = owners // 4
    clusters, width, panels = outgoing.shape
    block = (clusters // owners, width, panels)
    return pl.pallas_call(
        functools.partial(scatter_kernel, line),
        out_shape=jax.ShapeDtypeStruct(block, outgoing.dtype),
        in_specs=[pl.BlockSpec(memory_space=pl.ANY)],
        out_specs=pl.BlockSpec(memory_space=pltpu.VMEM),
        scratch_shapes=[
            pltpu.VMEM((2 * line,) + block, jnp.float32),
            pltpu.VMEM((2 * line,) + block, jnp.float32),
            pltpu.VMEM((line,) + block, jnp.float32),
            pltpu.VMEM((line,) + block, jnp.float32),
            pltpu.VMEM((line,) + block, jnp.float32),
            pltpu.SemaphoreType.DMA((4 * line,)),
            pltpu.SemaphoreType.DMA((2 * line,)),
            pltpu.SemaphoreType.DMA((2 * line,)),
            pltpu.SemaphoreType.DMA((line,)),
            pltpu.SemaphoreType.DMA((line,)),
            pltpu.SemaphoreType.DMA((line,)),
        ],
        compiler_params=pltpu.CompilerParams(
            collective_id=1, has_side_effects=True, vmem_limit_bytes=vmem_budget
        ),
        name="scatter_sums",
    )(outgoing)


def gather_shards(
    point_offsets,
    panel_normals,
    right_sketch,
    left_sketch,
    pair_count,
    pair_rows,
    pair_offset,
    pair_cols,
):
    owners = lax.axis_size("clus")
    position = lax.axis_index("clus")
    cl_dev, width, panels = right_sketch.shape
    spare = jnp.zeros((cl_dev, geometry_rows - 6, panels), jnp.float32)
    packed = jnp.concatenate([right_sketch, point_offsets, panel_normals, spare], axis=1)
    columns, features, left = gather_clusters(packed, left_sketch, owners)
    target = (position + 1 + pair_offset[:, 0]) % owners
    row_sum, outgoing = sketch_pairs(
        pair_count,
        pair_rows,
        position * cl_dev + pair_rows,
        target * cl_dev + pair_cols,
        features,
        left,
        columns,
        width,
    )
    col_sum = scatter_sums(outgoing, owners)
    return (row_sum, col_sum)


def shards(
    point_offsets,
    panel_normals,
    right_sketch,
    left_sketch,
    pair_count,
    pair_rows,
    pair_offset,
    pair_cols,
):
    cl_dev, width, panels = right_sketch.shape
    held = lax.axis_size("clus") * cl_dev * (2 * width + geometry_rows) * panels * 4
    fits = lax.axis_size("clus") == 16 and held + 2**23 <= vmem_budget
    plan = gather_shards if fits else exchange_shards
    return plan(
        point_offsets,
        panel_normals,
        right_sketch,
        left_sketch,
        pair_count,
        pair_rows,
        pair_offset,
        pair_cols,
    )


def solution(mesh):
    return jax.shard_map(
        shards,
        mesh=mesh,
        in_specs=(
            P(("groups", "clus"), None, None),
            P(("groups", "clus"), None, None),
            P(("groups", "clus"), None, None),
            P(("groups", "clus"), None, None),
            P(("groups", "clus")),
            P(("groups", "clus")),
            P(("groups", "clus"), None),
            P(("groups", "clus")),
        ),
        out_specs=(P(("groups", "clus"), None, None), P(("groups", "clus"), None, None)),
        check_vma=False,
    )
```
